256 devices in a mesh: col: 32 (over x, y, core), row: 4 (over z_lo), batch: 2 (over z_hi).
Axes of the slice: x: 4, y: 4, z: 8 (z_hi: 2, z_lo: 4; z = z_hi * 4 + z_lo), core: 2. Of those that a mesh axis runs over, the one named last changes fastest.
Arguments:
- checkpoint: bfloat16 [4, 32, 128, 8, 128], P('batch', 'col'), may hold values from -6 to 6
- peps: bfloat16 [4, 32, 2, 4096], P('row', 'col'), may hold values from -2 to 2
- configs: int32 [4, 4, 32], P('batch', 'row', 'col'), may hold values from 0 to 1
- isometries: bfloat16 [4, 4, 32, 128, 8, 128], P('batch', 'row', 'col'), may hold values from -0.1875 to 0.1875
- out_cotangent: bfloat16 [4, 32, 128, 8, 128], P('batch', 'col'), may hold values from -6 to 6
Outputs:
- peps_grad: float32 [4, 32, 2, 4096], P('row', 'col')
- iso_grad: float32 [4, 4, 32, 128, 8, 128], P('batch', 'row', 'col')
- row_cotangents: bfloat16 [4, 4, 32, 128, 8, 128], P('batch', 'row', 'col')
The draws below stay inside these ranges and needn't reach their ends.
All inputs are finite; a program needn't handle non-finite values.
Results may differ from the reference program's by a relative error of at most 0.023.
Values may be sent and summed in bfloat16 or wider, within the bound.
No kernel may reach another device: no remote copies, remote signals or barrier semaphores. Data moves between devices by JAX's collectives and lax.ppermute only.
A program may use at most 128 MiB of HBM per device.

```python
import jax
import jax.numpy as jnp

CHI = 128
D = 8
PHYS = 2
COLS = 32
ROWS = 4
SAMPLES = 4
QUAD = 4096


def set_ends(values, stream_key, low, top_value):
    longest = values.shape.index(max(values.shape))
    spots = []
    for shift in (0, 1):
        where = [jax.random.randint(jax.random.fold_in(stream_key, axis), (), 0, length) for axis, length in enumerate(values.shape)]
        where[longest] = (where[longest] + shift) % values.shape[longest]
        spots.append(tuple(where))
    return values.at[spots[0]].set(low).at[spots[1]].set(top_value)


def block_levels(key, extent, shards, smallest, top_value):
    level = 1.0
    for position, shards_of in shards:
        draws = jax.random.uniform(jax.random.fold_in(jax.random.fold_in(key, 6), position), (shards_of,), jnp.float32, smallest / len(shards), top_value / len(shards))
        level = level * jnp.repeat(jnp.exp(draws), extent[position] // shards_of).reshape((-1,) + (1,) * (len(extent) - 1 - position))
    return level


def scatter_about(rng, extent, scale, limit, shards=(), kind=jnp.bfloat16):
    entries = jax.random.normal(rng, extent, jnp.float32) * scale
    if len(shards) > 0:
        entries = block_levels(rng, extent, shards, -0.22, 0.18) * entries
    return jnp.clip(entries, min=-limit, max=limit).astype(kind)


def setup_inputs(seed: int = 0) -> dict:
    streams_of = jax.random.split(jax.random.key(seed), 6)
    return {
        "checkpoint": scatter_about(streams_of[0], (SAMPLES, COLS, CHI, D, CHI), 1.0, 6.0, ((0, 2), (1, 32))),
        "peps": scatter_about(streams_of[1], (ROWS, COLS, PHYS, QUAD), D ** -0.5, 2.0, ((0, 4), (1, 32))),
        "configs": set_ends(jax.random.randint(streams_of[2], (SAMPLES, ROWS, COLS), 0, PHYS), jax.random.fold_in(streams_of[2], 1), 0, PHYS - 1).astype(jnp.int32),
        "isometries": scatter_about(streams_of[3], (SAMPLES, ROWS, COLS, CHI, D, CHI), (CHI * D) ** -0.5, 0.1875, ((0, 2), (1, 4), (2, 32))),
        "out_cotangent": scatter_about(streams_of[4], (SAMPLES, COLS, CHI, D, CHI), 1.0, 6.0, ((0, 2), (1, 32))),
    }


def contract(form, left, right):
    return jnp.einsum(form, left.astype(jnp.float32), right.astype(jnp.float32))


def absorb_front(boundary, tiles, left_iso):
    lifted = contract('...alk,...aub->...lkub', left_iso, boundary).astype(jnp.bfloat16)
    spread = contract('...lkub,...lurd->...rdkb', lifted, tiles).astype(jnp.bfloat16)
    return lifted, spread


def absorb_close(spread, right_iso):
    return contract('...rdkb,...brj->...kdj', spread, right_iso).astype(jnp.bfloat16)


def absorb_back(boundary, tiles, left_iso, right_iso, lifted, spread, zbar):
    spread_bar = contract('...kdj,...brj->...rdkb', zbar, right_iso).astype(jnp.bfloat16)
    right_bar = contract('...rdkb,...kdj->...brj', spread, zbar)
    lifted_bar = contract('...rdkb,...lurd->...lkub', spread_bar, tiles).astype(jnp.bfloat16)
    tile_bar = contract('...lkub,...rdkb->...lurd', lifted, spread_bar)
    boundary_bar = contract('...alk,...lkub->...aub', left_iso, lifted_bar).astype(jnp.bfloat16)
    left_bar = contract('...aub,...lkub->...alk', boundary, lifted_bar)
    return boundary_bar, left_bar, right_bar, tile_bar


def reference(checkpoint, peps, configs, isometries, out_cotangent):
    levels = jnp.arange(PHYS, dtype=jnp.int32)
    right_all = jnp.roll(isometries, -1, axis=2)
    tile_grad = jnp.zeros((ROWS, COLS, PHYS, QUAD), jnp.float32)
    left_grads = []
    right_grads = []
    cotangent_list = []
    for sample in range(SAMPLES):
        select = (configs[sample][..., None] == levels).astype(jnp.float32)
        tiles = jnp.zeros((ROWS, COLS, QUAD), jnp.bfloat16)
        for level in range(PHYS):
            tiles = jnp.where(configs[sample][..., None] == level, peps[:, :, level], tiles)
        tiles = tiles.reshape((ROWS, COLS, D, D, D, D))
        inputs = [checkpoint[sample]]
        for row_at in range(ROWS - 1):
            lifted, spread = absorb_front(inputs[row_at], tiles[row_at], isometries[sample, row_at])
            inputs.append(absorb_close(spread, right_all[sample, row_at]))
        zbar = out_cotangent[sample]
        left_rows = [None] * ROWS
        right_rows = [None] * ROWS
        cot_rows = [None] * ROWS
        for row_at in range(ROWS - 1, -1, -1):
            lifted, spread = absorb_front(inputs[row_at], tiles[row_at], isometries[sample, row_at])
            boundary_bar, left_bar, right_bar, tile_bar = absorb_back(
                inputs[row_at], tiles[row_at], isometries[sample, row_at], right_all[sample, row_at], lifted, spread, zbar)
            left_rows[row_at] = left_bar
            right_rows[row_at] = right_bar
            cot_rows[row_at] = boundary_bar
            tile_grad = tile_grad.at[row_at].add(select[row_at][:, :, None] * tile_bar.reshape((COLS, 1, QUAD)))
            zbar = boundary_bar
        left_grads.append(jnp.stack(left_rows))
        right_grads.append(jnp.stack(right_rows))
        cotangent_list.append(jnp.stack(cot_rows))
    left_all = jnp.stack(left_grads)
    right_back = jnp.roll(jnp.stack(right_grads), 1, axis=2)
    iso_grad = left_all + right_back
    peps_grad = tile_grad * (1.0 / SAMPLES)
    return peps_grad, iso_grad, jnp.stack(cotangent_list)
```

```python
import functools

import jax
import jax.numpy as jnp
from jax import lax
from jax.experimental import pallas as pl
from jax.experimental.pallas import tpu as pltpu
from jax.sharding import PartitionSpec as P

F32 = jnp.float32
BF16 = jnp.bfloat16
D = 8
CHI = 128
GROUPS = CHI // D
ROWS = 4
NT = (((1,), (1,)), ((), ()))


def mm(a, b):
    return jnp.dot(a, b, preferred_element_type=F32)


def mm_nt(a, b):
    return lax.dot_general(a, b, NT, preferred_element_type=F32)


def lanes(parts):
    return jnp.concatenate(parts, axis=-1)


def swap_in(src, scratch, dst):
    scratch[...] = src[...].astype(F32).reshape(CHI * D, CHI)
    for leg in range(D):
        dst[leg] = scratch[pl.ds(leg, CHI, stride=D), :].astype(BF16)


def front(b, wlt, kron, x, y):
    left = wlt[...].reshape(D * CHI, CHI)
    for pair in range(D // 2):
        out = mm(left, lanes([b[2 * pair], b[2 * pair + 1]]))
        halves = [out[:, :CHI].reshape(D, GROUPS, D, CHI), out[:, CHI:].reshape(D, GROUPS, D, CHI)]
        both = jnp.concatenate(halves, axis=2).astype(BF16)
        for leg in range(D):
            x[:, leg, pair] = both[leg]

    def body(p, _):
        two = lanes([x[2 * p].reshape(512, CHI), x[2 * p + 1].reshape(512, CHI)])
        out = mm(kron[...], two).astype(BF16)
        y[2 * p] = out[:, :CHI].reshape(D, 64, CHI)
        y[2 * p + 1] = out[:, CHI:].reshape(D, 64, CHI)
        return 0

    lax.fori_loop(0, GROUPS // 2, body, 0, unroll=True)


def close(y, wr, z):
    left = lanes([y[:, r].reshape(D * CHI, CHI) for r in range(D)])
    out = mm(left, wr[...].reshape(D * CHI, CHI)).reshape(GROUPS, D, D, CHI)
    for d in range(D):
        z[d] = out[:, d].reshape(CHI, CHI).astype(BF16)


def back(zbar, wr, wl, kron_t, yb, xb, bbar):
    left = zbar[...].reshape(D * CHI, CHI)
    for pair in range(D // 2):
        out = mm_nt(left, wr[2 * pair : 2 * pair + 2].reshape(2 * CHI, CHI))
        for half in range(2):
            piece = out[:, half * CHI : (half + 1) * CHI].reshape(D, GROUPS, D, CHI)
            yb[:, 2 * pair + half] = jnp.swapaxes(piece, 0, 1).reshape(GROUPS, 64, CHI).astype(BF16)

    for p in range(GROUPS // 2):
        two = lanes([yb[2 * p].reshape(512, CHI), yb[2 * p + 1].reshape(512, CHI)])
        out = mm(kron_t[...], two)
        halves = [out[:, :CHI].reshape(D, D, D, CHI), out[:, CHI:].reshape(D, D, D, CHI)]
        xb[:, :, 16 * p : 16 * p + 16, :] = jnp.concatenate(halves, axis=2).astype(BF16)

    left = lanes([wl[leg] for leg in range(D)])
    for pair in range(D // 2):
        right = lanes([xb[:, 2 * pair].reshape(D * CHI, CHI), xb[:, 2 * pair + 1].reshape(D * CHI, CHI)])
        out = mm(left, right).astype(BF16)
        bbar[2 * pair] = out[:, :CHI]
        bbar[2 * pair + 1] = out[:, CHI:]


def right_grad(y, zbar, out_ref):
    z = zbar[...].astype(F32).reshape(D, GROUPS, D, CHI)
    z = jnp.swapaxes(z, 0, 1).reshape(D * CHI, CHI).T.astype(BF16)
    for pair in range(D // 2):
        right = lanes([y[:, 2 * pair].reshape(D * CHI, CHI), y[:, 2 * pair + 1].reshape(D * CHI, CHI)])
        out = mm(z, right).astype(BF16)
        out_ref[2 * pair] = out[:, :CHI]
        out_ref[2 * pair + 1] = out[:, CHI:]


def tile_grad(x, yb, acc, out_ref, state):
    for p in range(GROUPS // 2):
        left = lanes([x[2 * p].reshape(512, CHI), x[2 * p + 1].reshape(512, CHI)])
        right = lanes([yb[2 * p].reshape(512, CHI), yb[2 * p + 1].reshape(512, CHI)])
        out = mm_nt(left, right)
        if p == 0:
            acc[...] = out
        else:
            acc[...] += out
    sub = lax.broadcasted_iota(jnp.int32, (D, 512), 0)
    lane = lax.broadcasted_iota(jnp.int32, (D, 512), 1)
    keep = (sub == lane % D).astype(F32)
    rows = jnp.sum(acc[...].reshape(64, D, 512) * keep[None], axis=1)
    pick = (lax.broadcasted_iota(jnp.int32, (512, 64), 0) // D == lax.broadcasted_iota(jnp.int32, (512, 64), 1)).astype(F32)
    total = jnp.dot(rows, pick, preferred_element_type=F32, precision=lax.Precision.HIGHEST)
    for level in range(2):
        out_ref[level] = jnp.where(state == level, total, 0.0)


def left_grad(b, xb, out_ref):
    left = lanes([b[u] for u in range(D)])
    for pair in range(D // 2):
        right = jnp.concatenate(
            [lanes([xb[leg, u] for u in range(D)]) for leg in (2 * pair, 2 * pair + 1)], axis=0
        )
        out = mm_nt(left, right)
        out_ref[pl.ds(2 * pair, CHI, stride=D), :] = out[:, :CHI]
        out_ref[pl.ds(2 * pair + 1, CHI, stride=D), :] = out[:, CHI:]


def iso_kernel(w_ref, wl_ref, scratch):
    swap_in(w_ref, scratch, wl_ref)


def prep_kernel(states, w_refs, wl_refs, peps, ck, oc, wl1_ref, wlt_ref, start_ref, kron_ref, kron_t_ref, scratch):
    pass


def call(kernel, ins, outs, scratch=(), vmem=56):
    return pl.pallas_call(
        kernel,
        in_specs=[pl.BlockSpec(memory_space=pltpu.SMEM if i.dtype == jnp.int32 else pltpu.VMEM) for i in ins],
        out_specs=[pl.BlockSpec(memory_space=pltpu.VMEM) for _ in outs],
        out_shape=[jax.ShapeDtypeStruct(*o) for o in outs],
        scratch_shapes=list(scratch),
        compiler_params=pltpu.CompilerParams(vmem_limit_bytes=vmem << 20),
    )(*ins)


T = ((D, CHI, CHI), BF16)
XS = ((GROUPS, D, D // 2, 16, CHI), BF16)
YS = ((GROUPS, D, 64, CHI), BF16)
XBS = ((D, D, CHI, CHI), BF16)
RELAY = pltpu.VMEM((CHI * D, CHI), F32)


def turn_kernel(w_ref, wl_ref, scratch):
    swap_in(w_ref, scratch, wl_ref)


def prep(state, peps, wl, ck, oc, wlt, start, kron, kron_t, scratch):
    row = lax.axis_index("row")
    for leg in range(D):
        wlt[leg] = wl[leg].astype(F32).T.astype(BF16)
    site = jnp.where(state[0] == 0, peps[0].astype(F32), peps[1].astype(F32)).astype(BF16)
    wide = (lax.broadcasted_iota(jnp.int32, (512, 64), 0) // D == lax.broadcasted_iota(jnp.int32, (512, 64), 1)).astype(F32).astype(BF16)
    tall = (lax.broadcasted_iota(jnp.int32, (64, 512), 0) == lax.broadcasted_iota(jnp.int32, (64, 512), 1) // D).astype(F32).astype(BF16)
    keep = (lax.broadcasted_iota(jnp.int32, (512, 512), 0) % D == lax.broadcasted_iota(jnp.int32, (512, 512), 1) % D).astype(F32)
    rows = mm(wide, site).astype(BF16)
    kron_t[...] = (mm(rows, tall) * keep).astype(BF16)
    rows = mm(wide, site.astype(F32).T.astype(BF16)).astype(BF16)
    kron[...] = (mm(rows, tall) * keep).astype(BF16)

    @pl.when(row == 0)
    def _():
        swap_in(ck, scratch, start)

    @pl.when(row == ROWS - 1)
    def _():
        swap_in(oc, scratch, start)


def first_kernel(active, arrived, wl, wlt, wr, kron, kron_t, msg, s1, s2):
    row = lax.axis_index("row")

    @pl.when(row == active)
    def _():
        front(arrived, wlt, kron, s1.reshape(XS[0]), s2)
        close(s2, wr, msg)

    @pl.when(row == ROWS - 1 - active)
    def _():
        back(arrived, wr, wl, kron_t, s2, s1, msg)


def merge_rows(row, outer, inner):
    return jnp.where((row == 0) | (row == ROWS - 1), outer, inner)


def second_kernel(active, arrived, wl, wlt, wr, kron, kron_t, msg, s1, s2):
    row = lax.axis_index("row")

    @pl.when(row == active)
    def _():
        front(arrived, wlt, kron, s1.reshape(XS[0]), s2)
        if active < ROWS - 1:
            close(s2, wr, msg)

    @pl.when(row == ROWS - 1 - active)
    def _():
        back(arrived, wr, wl, kron_t, s2, s1, msg)


def grads(first, second, m_first, m_second, a1, a2, b1, b2, state, right, left, tiles, cot, acc, scratch):
    row = lax.axis_index("row")

    def work(boundary, zbar, bbar, x, y, xb, yb):
        right_grad(y, zbar, right)
        tile_grad(x, yb, acc, tiles, state[0])
        left_grad(boundary, xb, left)
        for leg in range(D):
            scratch[pl.ds(leg, CHI, stride=D), :] = bbar[leg].astype(F32)
        cot[...] = scratch[...].reshape(CHI, D, CHI).astype(BF16)

    @pl.when(row < ROWS // 2)
    def _():
        work(first, second, m_second, a1.reshape(XS[0]), a2, b1, b2)

    @pl.when(row >= ROWS // 2)
    def _():
        work(second, first, m_first, b1.reshape(XS[0]), b2, a1, a2)


def finish(left0, left1, got0, got1, out):
    for s, (left, got) in enumerate(((left0, got0), (left1, got1))):
        for leg in range(D):
            rows = pl.ds(leg, CHI, stride=D)
            out[s, rows, :] = left[rows, :] + got[leg].astype(F32).T


def shards(checkpoint, peps, configs, isometries, out_cotangent):
    samples = checkpoint.shape[0]
    row = lax.axis_index("row")
    cols = lax.axis_size("col")
    from_right = [((i + 1) % cols, i) for i in range(cols)]
    from_left = [(i, (i + 1) % cols) for i in range(cols)]
    outer = [(0, 1), (1, 0), (2, 3), (3, 2)]
    inner = [(1, 2), (2, 1)]
    swaps = [outer, inner, outer]
    site = peps.reshape(2, 64, 64)
    states = [configs[s, 0] for s in range(samples)]
    both = range(samples)
    wl = [call(turn_kernel, [isometries[s, 0, 0]], [T], [RELAY])[0] for s in both]
    wr = [lax.ppermute(wl[s], "col", from_right) for s in both]
    wlt, start, kron, kron_t = zip(*[
        call(prep, [states[s], site, wl[s], checkpoint[s, 0], out_cotangent[s, 0]],
             [T, T, ((512, 512), BF16), ((512, 512), BF16)], [RELAY])
        for s in both
    ])
    first_in = list(start)
    second_in = [None] * samples
    first_out = [None] * samples
    second_out = [None] * samples
    sent = [None] * samples
    for level in range(ROWS):
        for s in both:
            args = [wl[s], wlt[s], wr[s], kron[s], kron_t[s]]
            if level == 0:
                first_out[s] = call(functools.partial(first_kernel, 0), [start[s]] + args, [T, XBS, YS])
                sent[s] = lax.ppermute(first_out[s][0], "row", outer)
            elif level == 1:
                got = sent[s]
                other = call(functools.partial(first_kernel, 1), [got] + args, [T, XBS, YS])
                sent[s] = lax.ppermute(other[0], "row", inner)
                first_out[s] = [merge_rows(row, a, b) for a, b in zip(first_out[s], other)]
                first_in[s] = merge_rows(row, start[s], got)
            elif level == 2:
                second_in[s] = sent[s]
                second_out[s] = call(functools.partial(second_kernel, 2), [sent[s]] + args, [T, XBS, YS])
                sent[s] = lax.ppermute(second_out[s][0], "row", outer)
            else:
                other = call(functools.partial(second_kernel, 3), [sent[s]] + args, [T, XBS, YS])
                second_out[s] = [merge_rows(row, b, a) for a, b in zip(second_out[s], other)]
                second_in[s] = merge_rows(row, sent[s], second_in[s])
    right, left, tiles, cot = zip(*[
        call(grads,
             [first_in[s], second_in[s], first_out[s][0], second_out[s][0]] + list(first_out[s][1:]) + list(second_out[s][1:]) + [states[s]],
             [T, ((CHI * D, CHI), F32), ((2, 64, 64), F32), ((CHI, D, CHI), BF16)],
             [pltpu.VMEM((512, 512), F32), RELAY])
        for s in both
    ])
    got = [lax.ppermute(right[s], "col", from_left) for s in both]
    total = lax.psum(tiles[0] + tiles[1], "batch")
    iso_grad = call(finish, [left[0], left[1], got[0], got[1]], [((2, CHI * D, CHI), F32)])[0]
    peps_grad = (total * (1.0 / (samples * lax.axis_size("batch")))).reshape(1, 1, 2, 4096)
    return (peps_grad, iso_grad.reshape(2, 1, 1, CHI, D, CHI), jnp.stack(cot)[:, None, None])


def solution(mesh):
    in_specs = (
        P("batch", "col", None, None, None),
        P("row", "col", None, None),
        P("batch", "row", "col"),
        P("batch", "row", "col", None, None, None),
        P("batch", "col", None, None, None),
    )
    out_specs = (
        P("row", "col", None, None),
        P("batch", "row", "col", None, None, None),
        P("batch", "row", "col", None, None, None),
    )
    return jax.shard_map(shards, mesh=mesh, in_specs=in_specs, out_specs=out_specs, check_vma=False)
```

```python
import functools

import jax
import jax.numpy as jnp
from jax import lax
from jax.experimental import pallas as pl
from jax.experimental.pallas import tpu as pltpu
from jax.sharding import PartitionSpec as P

F32 = jnp.float32
BF16 = jnp.bfloat16
D = 8
CHI = 128
GROUPS = CHI // D
ROWS = 4
NT = (((1,), (1,)), ((), ()))


def mm(a, b):
    return jnp.dot(a, b, preferred_element_type=F32)


def mm_nt(a, b):
    return lax.dot_general(a, b, NT, preferred_element_type=F32)


def lanes(parts):
    return jnp.concatenate(parts, axis=-1)


def swap_in(src, scratch, dst):
    scratch[...] = src[...].astype(F32).reshape(CHI * D, CHI)
    for leg in range(D):
        dst[leg] = scratch[pl.ds(leg, CHI, stride=D), :].astype(BF16)


def front(b, wlt, kron, x, y):
    left = wlt[...].reshape(D * CHI, CHI)
    for pair in range(D // 2):
        out = mm(left, lanes([b[2 * pair], b[2 * pair + 1]]))
        halves = [out[:, :CHI].reshape(D, GROUPS, D, CHI), out[:, CHI:].reshape(D, GROUPS, D, CHI)]
        both = jnp.concatenate(halves, axis=2).astype(BF16)
        for leg in range(D):
            x[:, leg, pair] = both[leg]

    def body(p, _):
        two = lanes([x[2 * p].reshape(512, CHI), x[2 * p + 1].reshape(512, CHI)])
        out = mm(kron[...], two).astype(BF16)
        y[2 * p] = out[:, :CHI].reshape(D, 64, CHI)
        y[2 * p + 1] = out[:, CHI:].reshape(D, 64, CHI)
        return 0

    lax.fori_loop(0, GROUPS // 2, body, 0, unroll=True)


def close(y, wr, z):
    left = lanes([y[:, r].reshape(D * CHI, CHI) for r in range(D)])
    out = mm(left, wr[...].reshape(D * CHI, CHI)).reshape(GROUPS, D, D, CHI)
    for d in range(D):
        z[d] = out[:, d].reshape(CHI, CHI).astype(BF16)


def back_spread(zbar, wr, yb):
    left = zbar[...].reshape(D * CHI, CHI)
    for pair in range(D // 2):
        out = mm_nt(left, wr[2 * pair : 2 * pair + 2].reshape(2 * CHI, CHI))
        for half in range(2):
            piece = out[:, half * CHI : (half + 1) * CHI].reshape(D, GROUPS, D, CHI)
            yb[:, 2 * pair + half] = jnp.swapaxes(piece, 0, 1).reshape(GROUPS, 64, CHI).astype(BF16)


def back_lift(wl, kron_t, yb, xb, bbar):
    for p in range(GROUPS // 2):
        two = lanes([yb[2 * p].reshape(512, CHI), yb[2 * p + 1].reshape(512, CHI)])
        out = mm(kron_t[...], two)
        halves = [out[:, :CHI].reshape(D, D, D, CHI), out[:, CHI:].reshape(D, D, D, CHI)]
        xb[:, :, 16 * p : 16 * p + 16, :] = jnp.concatenate(halves, axis=2).astype(BF16)

    left = lanes([wl[leg] for leg in range(D)])
    for pair in range(D // 2):
        right = lanes([xb[:, 2 * pair].reshape(D * CHI, CHI), xb[:, 2 * pair + 1].reshape(D * CHI, CHI)])
        out = mm(left, right).astype(BF16)
        bbar[2 * pair] = out[:, :CHI]
        bbar[2 * pair + 1] = out[:, CHI:]


def back(zbar, wr, wl, kron_t, yb, xb, bbar):
    back_spread(zbar, wr, yb)
    back_lift(wl, kron_t, yb, xb, bbar)


def right_grad(y, zbar, out_ref):
    z = zbar[...].astype(F32).reshape(D, GROUPS, D, CHI)
    z = jnp.swapaxes(z, 0, 1).reshape(D * CHI, CHI).T.astype(BF16)
    for pair in range(D // 2):
        right = lanes([y[:, 2 * pair].reshape(D * CHI, CHI), y[:, 2 * pair + 1].reshape(D * CHI, CHI)])
        out = mm(z, right).astype(BF16)
        out_ref[2 * pair] = out[:, :CHI]
        out_ref[2 * pair + 1] = out[:, CHI:]


def tile_grad(x, yb, acc, out_ref, state):
    for p in range(GROUPS // 2):
        left = lanes([x[2 * p].reshape(512, CHI), x[2 * p + 1].reshape(512, CHI)])
        right = lanes([yb[2 * p].reshape(512, CHI), yb[2 * p + 1].reshape(512, CHI)])
        out = mm_nt(left, right)
        if p == 0:
            acc[...] = out
        else:
            acc[...] += out
    sub = lax.broadcasted_iota(jnp.int32, (D, 512), 0)
    lane = lax.broadcasted_iota(jnp.int32, (D, 512), 1)
    keep = (sub == lane % D).astype(F32)
    rows = jnp.sum(acc[...].reshape(64, D, 512) * keep[None], axis=1)
    pick = (lax.broadcasted_iota(jnp.int32, (512, 64), 0) // D == lax.broadcasted_iota(jnp.int32, (512, 64), 1)).astype(F32)
    total = jnp.dot(rows, pick, preferred_element_type=F32, precision=lax.Precision.HIGHEST)
    for level in range(2):
        out_ref[level] = jnp.where(state == level, total, 0.0)


def left_grad(b, xb, out_ref):
    left = lanes([b[u] for u in range(D)])
    for pair in range(D // 2):
        right = jnp.concatenate(
            [lanes([xb[leg, u] for u in range(D)]) for leg in (2 * pair, 2 * pair + 1)], axis=0
        )
        out = mm_nt(left, right)
        out_ref[pl.ds(2 * pair, CHI, stride=D), :] = out[:, :CHI]
        out_ref[pl.ds(2 * pair + 1, CHI, stride=D), :] = out[:, CHI:]


T = ((D, CHI, CHI), BF16)
XS = ((GROUPS, D, D // 2, 16, CHI), BF16)
YS = ((GROUPS, D, 64, CHI), BF16)
XBS = ((D, D, CHI, CHI), BF16)
KRON = ((512, 512), BF16)
RAW = pltpu.VMEM((CHI, D, CHI), BF16)
RELAY = pltpu.VMEM((CHI * D, CHI), F32)


def call(kernel, ins, outs, scratch=(), alias=None, vmem=20):
    specs, operands = [], []
    for i in ins:
        kind, array = i if isinstance(i, tuple) else (pltpu.VMEM, i)
        specs.append(pl.BlockSpec(memory_space=kind))
        operands.append(pltpu.with_memory_space_constraint(array, kind) if kind == pltpu.VMEM else array)
    out_specs, shapes = [], []
    for o in outs:
        kind, shape = o if len(o) == 2 and isinstance(o[1], tuple) else (pltpu.VMEM, o)
        out_specs.append(pl.BlockSpec(memory_space=kind))
        shapes.append(kind(*shape))
    return pl.pallas_call(
        kernel,
        in_specs=specs,
        out_specs=out_specs,
        out_shape=shapes,
        scratch_shapes=list(scratch),
        input_output_aliases=alias or {},
        compiler_params=pltpu.CompilerParams(vmem_limit_bytes=vmem << 20),
    )(*operands)


def turn(s, w, wl, wlt, raw, scratch, sem):
    copy = pltpu.make_async_copy(w.at[s, 0, 0], raw, sem)
    copy.start()
    copy.wait()
    swap_in(raw, scratch, wl)
    for leg in range(D):
        wlt[leg] = wl[leg].astype(F32).T.astype(BF16)


def prep(s, states, peps, ck, oc, start, kron, kron_t, raw, scratch, sem):
    row = lax.axis_index("row")
    sources = ((0, ck), (ROWS - 1, oc))
    for at, source in sources:

        @pl.when(row == at)
        def _():
            pltpu.make_async_copy(source.at[s, 0], raw, sem).start()

    site = jnp.where(states[s, 0, 0] == 0, peps[0].astype(F32), peps[1].astype(F32)).astype(BF16)
    wide = (lax.broadcasted_iota(jnp.int32, (512, 64), 0) // D == lax.broadcasted_iota(jnp.int32, (512, 64), 1)).astype(F32).astype(BF16)
    tall = (lax.broadcasted_iota(jnp.int32, (64, 512), 0) == lax.broadcasted_iota(jnp.int32, (64, 512), 1) // D).astype(F32).astype(BF16)
    keep = (lax.broadcasted_iota(jnp.int32, (512, 512), 0) % D == lax.broadcasted_iota(jnp.int32, (512, 512), 1) % D).astype(F32)
    rows = mm(wide, site).astype(BF16)
    kron_t[...] = (mm(rows, tall) * keep).astype(BF16)
    rows = mm(wide, site.astype(F32).T.astype(BF16)).astype(BF16)
    kron[...] = (mm(rows, tall) * keep).astype(BF16)
    for at, source in sources:

        @pl.when(row == at)
        def _():
            pltpu.make_async_copy(source.at[s, 0], raw, sem).wait()
            swap_in(raw, scratch, start)


def absorb(level, *refs):
    arrived, wl, wlt, wr, kron, kron_t = refs[:6]
    x, y, xb, yb, msg = refs[-5:]
    row = lax.axis_index("row")

    @pl.when(row == level)
    def _():
        front(arrived, wlt, kron, x, y)
        close(y, wr, msg)

    @pl.when(row == ROWS - 1 - level)
    def _():
        back(arrived, wr, wl, kron_t, yb, xb, msg)


def meet(start, got0, got1, got2, wlt, kron, x_in, y_in, x, y, right, bnd, zbar):
    row = lax.axis_index("row")
    first = [start, got0, got0, start]
    second = [got2, got1, got1, got2]
    for at in range(ROWS):

        @pl.when(row == at)
        def _():
            b, z = (first, second) if at < ROWS // 2 else (second, first)
            bnd[...] = b[at][...]
            zbar[...] = z[at][...]

    @pl.when(row == ROWS - 1)
    def _():
        front(bnd, wlt, kron, x, y)

    right_grad(y, zbar, right)


def tile_part(s, states, zbar, wr, x, xb_in, yb_in, *refs):
    tiles, yb, acc = refs[-3:]
    row = lax.axis_index("row")

    @pl.when(row == 0)
    def _():
        back_spread(zbar, wr, yb)

    tile_grad(x, yb, acc, tiles, states[s, 0, 0])
    if len(refs) == 4:
        tiles[...] += refs[0][...]


def rest(s, wl, kron_t, bnd, yb, msg0, msg1, msg2, *refs):
    xb, left, cot, msg, scratch, out, sem = refs[-7:]
    row = lax.axis_index("row")
    for at, source in ((1, msg2), (2, msg1), (3, msg0)):

        @pl.when(row == at)
        def _():
            msg[...] = source[...]

    @pl.when(row == 0)
    def _():
        back_lift(wl, kron_t, yb, xb, msg)

    for leg in range(D):
        scratch[pl.ds(leg, CHI, stride=D), :] = msg[leg].astype(F32)
    out[...] = scratch[...].reshape(CHI, D, CHI).astype(BF16)
    copy = pltpu.make_async_copy(out, cot.at[s, 0, 0], sem)
    copy.start()
    left_grad(bnd, xb, left)
    copy.wait()


def finish(s, left, got, *refs):
    out, total, sem = refs[-3:]
    for leg in range(D):
        rows = pl.ds(leg, CHI, stride=D)
        total[rows, :] = left[rows, :] + got[leg].astype(F32).T
    copy = pltpu.make_async_copy(total, out.at[s, 0, 0], sem)
    copy.start()
    copy.wait()


def shards(checkpoint, peps, configs, isometries, out_cotangent):
    samples = checkpoint.shape[0]
    cols = lax.axis_size("col")
    from_right = [((i + 1) % cols, i) for i in range(cols)]
    from_left = [(i, (i + 1) % cols) for i in range(cols)]
    outer = [(0, 1), (1, 0), (2, 3), (3, 2)]
    inner = [(1, 2), (2, 1)]
    swaps = [outer, inner, outer]
    site = peps.reshape(2, 64, 64)
    states = (pltpu.SMEM, configs)
    both = range(samples)
    dma = pltpu.SemaphoreType.DMA
    wl, wlt, wr = [None] * samples, [None] * samples, [None] * samples
    for s in both:
        wl[s], wlt[s] = call(functools.partial(turn, s), [(pl.ANY, isometries)], [T, T], [RAW, RELAY, dma])
        wr[s] = lax.ppermute(wl[s], "col", from_right)
    start, kron, kron_t = zip(*[
        call(functools.partial(prep, s), [states, site, (pl.ANY, checkpoint), (pl.ANY, out_cotangent)],
             [T, KRON, KRON], [RAW, RELAY, dma])
        for s in both
    ])
    stash = [[] for _ in both]
    got = [[start[s]] for s in both]
    msgs = [[] for _ in both]
    for level in range(ROWS - 1):
        for s in both:
            *stash[s], msg = call(
                functools.partial(absorb, level),
                [got[s][level], wl[s], wlt[s], wr[s], kron[s], kron_t[s]] + stash[s],
                [XS, YS, XBS, YS, T],
                alias={6 + i: i for i in range(len(stash[s]))},
            )
            msgs[s].append(msg)
            got[s].append(lax.ppermute(msg, "row", swaps[level]))
    tiles, cot, iso_grad, moved, left = [], [], [], [None] * samples, [None] * samples
    for s in both:
        x, y, xb, yb = stash[s]
        x, y, right, bnd, zbar = call(
            meet, got[s] + [wlt[s], kron[s], x, y], [XS, YS, T, T, T], alias={6: 0, 7: 1})
        moved[s] = lax.ppermute(right, "col", from_left)
        part, yb = call(
            functools.partial(tile_part, s), [states, zbar, wr[s], x, xb, yb] + tiles,
            [((2, 64, 64), F32), YS], [pltpu.VMEM((512, 512), F32)], alias={5: 1})
        tiles = [part]
        xb, left[s], *cot = call(
            functools.partial(rest, s), [wl[s], kron_t[s], bnd, yb] + msgs[s] + [xb] + cot_in(cot),
            [XBS, ((CHI * D, CHI), F32), (pltpu.HBM, ((2, 1, 1, CHI, D, CHI), BF16))],
            [pltpu.VMEM(*T), RELAY, RAW, dma], alias={7: 0} | ({8: 2} if cot else {}))
    total = tiles[0] + lax.ppermute(tiles[0], "batch", [(0, 1), (1, 0)])
    for s in both:
        iso_grad = call(
            functools.partial(finish, s), [left[s], moved[s]] + cot_in(iso_grad),
            [(pltpu.HBM, ((2, 1, 1, CHI * D, CHI), F32))], [RELAY, dma], alias={2: 0} if iso_grad else {})
    peps_grad = (total * (1.0 / (samples * lax.axis_size("batch")))).reshape(1, 1, 2, 4096)
    return (peps_grad, iso_grad[0].reshape(2, 1, 1, CHI, D, CHI), cot[0])


def cot_in(arrays):
    return [(pltpu.HBM, a) for a in arrays]


def solution(mesh):
    in_specs = (
        P("batch", "col", None, None, None),
        P("row", "col", None, None),
        P("batch", "row", "col"),
        P("batch", "row", "col", None, None, None),
        P("batch", "col", None, None, None),
    )
    out_specs = (
        P("row", "col", None, None),
        P("batch", "row", "col", None, None, None),
        P("batch", "row", "col", None, None, None),
    )
    return jax.shard_map(shards, mesh=mesh, in_specs=in_specs, out_specs=out_specs, check_vma=False)
```

```python
import functools

import jax
import jax.numpy as jnp
from jax import lax
from jax.experimental import pallas as pl
from jax.experimental.pallas import tpu as pltpu
from jax.sharding import PartitionSpec as P

F32 = jnp.float32
BF16 = jnp.bfloat16
D = 8
CHI = 128
GROUPS = CHI // D
ROWS = 4
NT = (((1,), (1,)), ((), ()))


def mm(a, b):
    return jnp.dot(a, b, preferred_element_type=F32)


def mm_nt(a, b):
    return lax.dot_general(a, b, NT, preferred_element_type=F32)


def lanes(parts):
    return jnp.concatenate(parts, axis=-1)


def picker(rows, columns, rule):
    i = lax.broadcasted_iota(jnp.int32, (rows, columns), 0)
    j = lax.broadcasted_iota(jnp.int32, (rows, columns), 1)
    return rule(i, j).astype(F32).astype(BF16)


def swap_in(src, scratch, dst):
    scratch[...] = src[...].astype(F32).reshape(CHI * D, CHI)
    for leg in range(D):
        dst[leg] = scratch[pl.ds(leg, CHI, stride=D), :].astype(BF16)


def front(b, wlt, kron, x, y):
    left = wlt[...].reshape(D * CHI, CHI)
    for pair in range(D // 2):
        out = mm(left, lanes([b[2 * pair], b[2 * pair + 1]]))
        halves = [out[:, :CHI].reshape(D, GROUPS, D, CHI), out[:, CHI:].reshape(D, GROUPS, D, CHI)]
        both = jnp.concatenate(halves, axis=2).astype(BF16)
        for leg in range(D):
            x[:, leg, pair] = both[leg]

    def body(p, _):
        two = lanes([x[2 * p].reshape(512, CHI), x[2 * p + 1].reshape(512, CHI)])
        out = mm(kron[...], two).astype(BF16)
        y[2 * p] = out[:, :CHI].reshape(D, 64, CHI)
        y[2 * p + 1] = out[:, CHI:].reshape(D, 64, CHI)
        return 0

    lax.fori_loop(0, GROUPS // 2, body, 0, unroll=True)


def close(y, wr, z):
    left = lanes([y[:, r].reshape(D * CHI, CHI) for r in range(D)])
    out = mm(left, wr[...].reshape(D * CHI, CHI)).reshape(GROUPS, D, D, CHI)
    for d in range(D):
        z[d] = out[:, d].reshape(CHI, CHI).astype(BF16)


def back_spread(zbar, wr, yb):
    left = zbar[...].reshape(D * CHI, CHI)
    for pair in range(D // 2):
        out = mm_nt(left, wr[2 * pair : 2 * pair + 2].reshape(2 * CHI, CHI))
        for half in range(2):
            piece = out[:, half * CHI : (half + 1) * CHI].reshape(D, GROUPS, D, CHI)
            yb[:, 2 * pair + half] = jnp.swapaxes(piece, 0, 1).reshape(GROUPS, 64, CHI).astype(BF16)


def back_lift(wl, kron_t, yb, xb, bbar):
    for p in range(GROUPS // 2):
        two = lanes([yb[2 * p].reshape(512, CHI), yb[2 * p + 1].reshape(512, CHI)])
        out = mm(kron_t[...], two)
        halves = [out[:, :CHI].reshape(D, D, D, CHI), out[:, CHI:].reshape(D, D, D, CHI)]
        xb[:, :, 16 * p : 16 * p + 16, :] = jnp.concatenate(halves, axis=2).astype(BF16)

    left = lanes([wl[leg] for leg in range(D)])
    for pair in range(D // 2):
        right = lanes([xb[:, 2 * pair].reshape(D * CHI, CHI), xb[:, 2 * pair + 1].reshape(D * CHI, CHI)])
        out = mm(left, right).astype(BF16)
        bbar[2 * pair] = out[:, :CHI]
        bbar[2 * pair + 1] = out[:, CHI:]


def back(zbar, wr, wl, kron_t, yb, xb, bbar):
    back_spread(zbar, wr, yb)
    back_lift(wl, kron_t, yb, xb, bbar)


def right_grad(y, zbar, out_ref):
    z = zbar[...].astype(F32).reshape(D, GROUPS, D, CHI)
    z = jnp.swapaxes(z, 0, 1).reshape(D * CHI, CHI).T.astype(BF16)
    for pair in range(D // 2):
        right = lanes([y[:, 2 * pair].reshape(D * CHI, CHI), y[:, 2 * pair + 1].reshape(D * CHI, CHI)])
        out = mm(z, right).astype(BF16)
        out_ref[2 * pair] = out[:, :CHI]
        out_ref[2 * pair + 1] = out[:, CHI:]


def tile_grad(x, yb, out_ref, state):
    sub = lax.broadcasted_iota(jnp.int32, (D, 256), 0)
    keep = (sub == lax.broadcasted_iota(jnp.int32, (D, 256), 1) % D).astype(F32)
    left = lanes([x[g].reshape(512, CHI) for g in range(GROUPS)])
    total = jnp.zeros((32, CHI), F32)
    for half in range(2):
        right = lanes([yb[g, 4 * half : 4 * half + 4].reshape(256, CHI) for g in range(GROUPS)])
        out = mm_nt(left, right).reshape(32, 2, D, 256) * keep[None, None]
        for odd in range(2):
            rows = jnp.sum(out[:, odd], axis=1)
            i = lax.broadcasted_iota(jnp.int32, (256, CHI), 0)
            j = lax.broadcasted_iota(jnp.int32, (256, CHI), 1)
            pick = (i // D + 32 * half + 64 * odd == j).astype(F32)
            total += jnp.dot(rows, pick, preferred_element_type=F32, precision=lax.Precision.HIGHEST)
    for level in range(2):
        out_ref[:, level, :] = jnp.where(state == level, total, 0.0)


def left_grad(b, xb, out_ref):
    left = lanes([b[u] for u in range(D)])
    for pair in range(D // 2):
        right = jnp.concatenate(
            [lanes([xb[leg, u] for u in range(D)]) for leg in (2 * pair, 2 * pair + 1)], axis=0
        )
        out = mm_nt(left, right)
        out_ref[pl.ds(2 * pair, CHI, stride=D), :] = out[:, :CHI]
        out_ref[pl.ds(2 * pair + 1, CHI, stride=D), :] = out[:, CHI:]


T = ((D, CHI, CHI), BF16)
XS = ((GROUPS, D, D // 2, 16, CHI), BF16)
YS = ((GROUPS, D, 64, CHI), BF16)
XBS = ((D, D, CHI, CHI), BF16)
KRON = ((512, 512), BF16)
RAW = pltpu.VMEM((CHI, D, CHI), BF16)
RELAY = pltpu.VMEM((CHI * D, CHI), F32)


class Chain:
    def __init__(self):
        self.link = None

    def __call__(self, kernel, ins, outs, scratch=(), alias=None, vmem=20, us=2.5):
        specs, operands = [], []
        alias = dict(alias or {})
        count = len(ins)
        if self.link is not None:
            ins = list(ins) + [self.link]
            alias[count] = len(outs)
        outs = list(outs) + [((8, 128), F32)]
        linked = len(ins) - count
        for i in ins:
            kind, array = i if isinstance(i, tuple) else (pltpu.VMEM, i)
            specs.append(pl.BlockSpec(memory_space=kind))
            operands.append(array if kind == pltpu.SMEM else pltpu.with_memory_space_constraint(array, kind))
        out_specs, shapes = [], []
        for o in outs:
            kind, shape = o if len(o) == 2 and isinstance(o[1], tuple) else (pltpu.VMEM, o)
            out_specs.append(pl.BlockSpec(memory_space=kind))
            shapes.append(kind(*shape))

        def body(*refs):
            after = count + linked
            kernel(*refs[:count], *refs[after : after + len(outs) - 1], *refs[after + len(outs) :])

        *results, self.link = pl.pallas_call(
            body,
            in_specs=specs,
            out_specs=out_specs,
            out_shape=shapes,
            scratch_shapes=list(scratch),
            input_output_aliases=alias,
            cost_estimate=pl.CostEstimate(flops=int(us * 1.15e9), bytes_accessed=0, transcendentals=0),
            compiler_params=pltpu.CompilerParams(vmem_limit_bytes=vmem << 20),
        )(*operands)
        return results


def turn(s, w, wl, wlt, raw, scratch, sem):
    copy = pltpu.make_async_copy(w.at[s, 0, 0], raw, sem)
    copy.start()
    copy.wait()
    swap_in(raw, scratch, wl)
    for leg in range(D):
        wlt[leg] = wl[leg].astype(F32).T.astype(BF16)


def prep(s, states, peps, ck, oc, start, kron, kron_t, raw, scratch, sem):
    row = lax.axis_index("row")
    sources = ((0, ck), (ROWS - 1, oc))
    for at, source in sources:

        @pl.when(row == at)
        def _():
            pltpu.make_async_copy(source.at[s, 0], raw, sem).start()

    site = jnp.where(states[s, 0, 0] == 0, peps[:, 0].astype(F32), peps[:, 1].astype(F32)).astype(BF16)
    keep = (lax.broadcasted_iota(jnp.int32, (D, 512), 0) == lax.broadcasted_iota(jnp.int32, (D, 512), 1) % D).astype(F32)
    wide = picker(512, 64, lambda i, j: i // D == j)
    tall = picker(64, 512, lambda i, j: i == j // D)
    rows, columns = 0.0, 0.0
    for half in range(2):
        part = site[:, 64 * half : 64 * half + 64]
        rows += mm(picker(512, 32, lambda i, j: i // D == 2 * j + half), part)
        columns += mm(part.astype(F32).T.astype(BF16), picker(32, 512, lambda i, j: 2 * i + half == j // D))
    kron_t[...] = (mm(rows.astype(BF16), tall).reshape(64, D, 512) * keep[None]).reshape(512, 512).astype(BF16)
    kron[...] = (mm(wide, columns.astype(BF16)).reshape(64, D, 512) * keep[None]).reshape(512, 512).astype(BF16)
    for at, source in sources:

        @pl.when(row == at)
        def _():
            pltpu.make_async_copy(source.at[s, 0], raw, sem).wait()
            swap_in(raw, scratch, start)


def absorb(level, *refs):
    arrived, wl, wlt, wr, kron, kron_t = refs[:6]
    x, y, xb, yb, msg = refs[-5:]
    row = lax.axis_index("row")

    @pl.when(row == level)
    def _():
        front(arrived, wlt, kron, x, y)
        close(y, wr, msg)

    @pl.when(row == ROWS - 1 - level)
    def _():
        back(arrived, wr, wl, kron_t, yb, xb, msg)


def meet(start, got0, got1, got2, wlt, kron, x_in, y_in, x, y, right, bnd, zbar):
    row = lax.axis_index("row")
    first = [start, got0, got0, start]
    second = [got2, got1, got1, got2]
    for at in range(ROWS):

        @pl.when(row == at)
        def _():
            b, z = (first, second) if at < ROWS // 2 else (second, first)
            bnd[...] = b[at][...]
            zbar[...] = z[at][...]

    @pl.when(row == ROWS - 1)
    def _():
        front(bnd, wlt, kron, x, y)

    right_grad(y, zbar, right)


def tile_part(s, states, zbar, wr, x, xb_in, yb_in, *refs):
    tiles, yb = refs[-2:]
    row = lax.axis_index("row")

    @pl.when(row == 0)
    def _():
        back_spread(zbar, wr, yb)

    tile_grad(x, yb, tiles, states[s, 0, 0])
    if len(refs) == 3:
        tiles[...] += refs[0][...]


def rest(s, wl, kron_t, bnd, yb, msg0, msg1, msg2, *refs):
    xb, left, cot, msg, scratch, out, sem = refs[-7:]
    row = lax.axis_index("row")
    for at, source in ((1, msg2), (2, msg1), (3, msg0)):

        @pl.when(row == at)
        def _():
            msg[...] = source[...]

    @pl.when(row == 0)
    def _():
        back_lift(wl, kron_t, yb, xb, msg)

    for leg in range(D):
        scratch[pl.ds(leg, CHI, stride=D), :] = msg[leg].astype(F32)
    out[...] = scratch[...].reshape(CHI, D, CHI).astype(BF16)
    copy = pltpu.make_async_copy(out, cot.at[s, 0, 0], sem)
    copy.start()
    left_grad(bnd, xb, left)
    copy.wait()


def finish(s, left, got, *refs):
    out, total, sem = refs[-3:]
    for leg in range(D):
        rows = pl.ds(leg, CHI, stride=D)
        total[rows, :] = left[rows, :] + got[leg].astype(F32).T
    copy = pltpu.make_async_copy(total, out.at[s, 0, 0], sem)
    copy.start()
    copy.wait()


def shards(checkpoint, peps, configs, isometries, out_cotangent):
    samples = checkpoint.shape[0]
    cols = lax.axis_size("col")
    from_right = [((i + 1) % cols, i) for i in range(cols)]
    from_left = [(i, (i + 1) % cols) for i in range(cols)]
    outer = [(0, 1), (1, 0), (2, 3), (3, 2)]
    depth = lax.axis_size("row") * lax.axis_size("batch")
    place = [(z % ROWS) * lax.axis_size("batch") + z // ROWS for z in range(depth)]
    inner = []
    for z in range(1, depth, 2):
        inner += [(place[z], place[(z + 1) % depth]), (place[(z + 1) % depth], place[z])]
    swaps = [("row", outer), (("row", "batch"), inner), ("row", outer)]
    site = jnp.swapaxes(peps.reshape(2, 32, 128), 0, 1)
    states = (pltpu.SMEM, configs)
    both = range(samples)
    call = Chain()
    dma = pltpu.SemaphoreType.DMA
    wl, wlt, wr = [None] * samples, [None] * samples, [None] * samples
    for s in both:
        wl[s], wlt[s] = call(functools.partial(turn, s), [(pltpu.HBM, isometries)], [T, T], [RAW, RELAY, dma])
        wr[s] = lax.ppermute(wl[s], "col", from_right)
    start, kron, kron_t = zip(*[
        call(functools.partial(prep, s), [states, site, (pltpu.HBM, checkpoint), (pltpu.HBM, out_cotangent)],
             [T, KRON, KRON], [RAW, RELAY, dma])
        for s in both
    ])
    stash = [[] for _ in both]
    got = [[start[s]] for s in both]
    msgs = [[] for _ in both]
    for level in range(ROWS - 1):
        for s in both:
            *stash[s], msg = call(
                functools.partial(absorb, level),
                [got[s][level], wl[s], wlt[s], wr[s], kron[s], kron_t[s]] + stash[s],
                [XS, YS, XBS, YS, T],
                alias={6 + i: i for i in range(len(stash[s]))},
            )
            msgs[s].append(msg)
            got[s].append(lax.ppermute(msg, *swaps[level]))
    tiles, cot, iso_grad, moved, left = [], [], [], [None] * samples, [None] * samples
    for s in both:
        x, y, xb, yb = stash[s]
        x, y, right, bnd, zbar = call(
            meet, got[s] + [wlt[s], kron[s], x, y], [XS, YS, T, T, T], alias={6: 0, 7: 1})
        moved[s] = lax.ppermute(right, "col", from_left)
        part, yb = call(
            functools.partial(tile_part, s), [states, zbar, wr[s], x, xb, yb] + tiles,
            [((32, 2, 128), F32), YS], alias={5: 1})
        tiles = [part]
        xb, left[s], *cot = call(
            functools.partial(rest, s), [wl[s], kron_t[s], bnd, yb] + msgs[s] + [xb] + cot_in(cot),
            [XBS, ((CHI * D, CHI), F32), (pltpu.HBM, ((2, 1, 1, CHI, D, CHI), BF16))],
            [pltpu.VMEM(*T), RELAY, RAW, dma], alias={7: 0} | ({8: 2} if cot else {}))
    total = tiles[0] + lax.ppermute(tiles[0], "batch", [(0, 1), (1, 0)])
    for s in both:
        iso_grad = call(
            functools.partial(finish, s), [left[s], moved[s]] + cot_in(iso_grad),
            [(pltpu.HBM, ((2, 1, 1, CHI * D, CHI), F32))], [RELAY, dma], alias={2: 0} if iso_grad else {})
    peps_grad = jnp.swapaxes(total * (1.0 / (samples * lax.axis_size("batch"))), 0, 1).reshape(1, 1, 2, 4096)
    return (peps_grad, iso_grad[0].reshape(2, 1, 1, CHI, D, CHI), cot[0])


def cot_in(arrays):
    return [(pltpu.HBM, a) for a in arrays]


def solution(mesh):
    in_specs = (
        P("batch", "col", None, None, None),
        P("row", "col", None, None),
        P("batch", "row", "col"),
        P("batch", "row", "col", None, None, None),
        P("batch", "col", None, None, None),
    )
    out_specs = (
        P("row", "col", None, None),
        P("batch", "row", "col", None, None, None),
        P("batch", "row", "col", None, None, None),
    )
    return jax.shard_map(shards, mesh=mesh, in_specs=in_specs, out_specs=out_specs, check_vma=False)
```

```python
import functools

import jax
import jax.numpy as jnp
from jax import lax
from jax.experimental import pallas as pl
from jax.experimental.pallas import tpu as pltpu
from jax.sharding import PartitionSpec as P

F32 = jnp.float32
BF16 = jnp.bfloat16
D = 8
CHI = 128
GROUPS = CHI // D
ROWS = 4
NT = (((1,), (1,)), ((), ()))


def mm(a, b):
    return jnp.dot(a, b, preferred_element_type=F32)


def mm_nt(a, b):
    return lax.dot_general(a, b, NT, preferred_element_type=F32)


def lanes(parts):
    return jnp.concatenate(parts, axis=-1)


def picker(rows, columns, rule):
    i = lax.broadcasted_iota(jnp.int32, (rows, columns), 0)
    j = lax.broadcasted_iota(jnp.int32, (rows, columns), 1)
    return rule(i, j).astype(F32).astype(BF16)


def swap_in(src, scratch, dst):
    scratch[...] = src[...].astype(F32).reshape(CHI * D, CHI)
    for leg in range(D):
        dst[leg] = scratch[pl.ds(leg, CHI, stride=D), :].astype(BF16)


def front(b, wlt, kron, x, y):
    left = wlt[...].reshape(D * CHI, CHI)
    for pair in range(D // 2):
        out = mm(left, lanes([b[2 * pair], b[2 * pair + 1]]))
        halves = [out[:, :CHI].reshape(D, GROUPS, D, CHI), out[:, CHI:].reshape(D, GROUPS, D, CHI)]
        both = jnp.concatenate(halves, axis=2).astype(BF16)
        for leg in range(D):
            x[:, leg, pair] = both[leg]

    def body(p, _):
        two = lanes([x[2 * p].reshape(512, CHI), x[2 * p + 1].reshape(512, CHI)])
        out = mm(kron[...], two).astype(BF16)
        y[2 * p] = out[:, :CHI].reshape(D, 64, CHI)
        y[2 * p + 1] = out[:, CHI:].reshape(D, 64, CHI)
        return 0

    lax.fori_loop(0, GROUPS // 2, body, 0, unroll=True)


def close(y, wr, z):
    left = lanes([y[:, r].reshape(D * CHI, CHI) for r in range(D)])
    out = mm(left, wr[...].reshape(D * CHI, CHI)).reshape(GROUPS, D, D, CHI)
    for d in range(D):
        z[d] = out[:, d].reshape(CHI, CHI).astype(BF16)


def back_spread(zbar, wr, yb):
    left = zbar[...].reshape(D * CHI, CHI)
    for pair in range(D // 2):
        out = mm_nt(left, wr[2 * pair : 2 * pair + 2].reshape(2 * CHI, CHI))
        for half in range(2):
            piece = out[:, half * CHI : (half + 1) * CHI].reshape(D, GROUPS, D, CHI)
            yb[:, 2 * pair + half] = jnp.swapaxes(piece, 0, 1).reshape(GROUPS, 64, CHI).astype(BF16)


def back_lift(wl, kron_t, yb, xb, bbar):
    for p in range(GROUPS // 2):
        two = lanes([yb[2 * p].reshape(512, CHI), yb[2 * p + 1].reshape(512, CHI)])
        out = mm(kron_t[...], two)
        halves = [out[:, :CHI].reshape(D, D, D, CHI), out[:, CHI:].reshape(D, D, D, CHI)]
        xb[:, :, 16 * p : 16 * p + 16, :] = jnp.concatenate(halves, axis=2).astype(BF16)

    left = lanes([wl[leg] for leg in range(D)])
    for pair in range(D // 2):
        right = lanes([xb[:, 2 * pair].reshape(D * CHI, CHI), xb[:, 2 * pair + 1].reshape(D * CHI, CHI)])
        out = mm(left, right).astype(BF16)
        bbar[2 * pair] = out[:, :CHI]
        bbar[2 * pair + 1] = out[:, CHI:]


def back(zbar, wr, wl, kron_t, yb, xb, bbar):
    back_spread(zbar, wr, yb)
    back_lift(wl, kron_t, yb, xb, bbar)


def right_grad(y, zbar, out_ref):
    z = zbar[...].astype(F32).reshape(D, GROUPS, D, CHI)
    z = jnp.swapaxes(z, 0, 1).reshape(D * CHI, CHI).T.astype(BF16)
    for pair in range(D // 2):
        right = lanes([y[:, 2 * pair].reshape(D * CHI, CHI), y[:, 2 * pair + 1].reshape(D * CHI, CHI)])
        out = mm(z, right).astype(BF16)
        out_ref[2 * pair] = out[:, :CHI]
        out_ref[2 * pair + 1] = out[:, CHI:]


def tile_grad(x, yb, out_ref, state):
    sub = lax.broadcasted_iota(jnp.int32, (D, 256), 0)
    keep = (sub == (lax.broadcasted_iota(jnp.int32, (D, 256), 1) & 7)).astype(F32)
    left = lanes([x[g].reshape(512, CHI) for g in range(GROUPS)])
    diagonal = []
    for half in range(2):
        right = lanes([yb[g, 4 * half : 4 * half + 4].reshape(256, CHI) for g in range(GROUPS)])
        out = mm_nt(left, right).reshape(32, 2, D, 256) * keep[None, None]
        diagonal.append([jnp.sum(out[:, odd], axis=1) for odd in range(2)])
    total = jnp.zeros((32, CHI), F32)
    for odd in range(2):
        rows = lanes([diagonal[0][odd], diagonal[1][odd]])
        high = rows.astype(BF16)
        low = (rows - high.astype(F32)).astype(BF16)
        pick = picker(512, CHI, lambda i, j: (i >> 3) + 64 * odd == j)
        total += mm(high, pick) + mm(low, pick)
    for level in range(2):
        out_ref[:, level, :] = jnp.where(state == level, total, 0.0)


def left_grad(b, xb, out_ref):
    left = lanes([b[u] for u in range(D)])
    for pair in range(D // 2):
        right = jnp.concatenate(
            [lanes([xb[leg, u] for u in range(D)]) for leg in (2 * pair, 2 * pair + 1)], axis=0
        )
        out = mm_nt(left, right)
        out_ref[pl.ds(2 * pair, CHI, stride=D), :] = out[:, :CHI]
        out_ref[pl.ds(2 * pair + 1, CHI, stride=D), :] = out[:, CHI:]


T = ((D, CHI, CHI), BF16)
XS = ((GROUPS, D, D // 2, 16, CHI), BF16)
YS = ((GROUPS, D, 64, CHI), BF16)
XBS = ((D, D, CHI, CHI), BF16)
KRON = ((512, 512), BF16)
RAW = pltpu.VMEM((CHI, D, CHI), BF16)
RELAY = pltpu.VMEM((CHI * D, CHI), F32)


class Chain:
    def __init__(self):
        self.link = None

    def __call__(self, kernel, ins, outs, scratch=(), alias=None, vmem=20, us=0.5):
        specs, operands = [], []
        alias = dict(alias or {})
        count = len(ins)
        if self.link is not None:
            ins = list(ins) + [self.link]
            alias[count] = len(outs)
        outs = list(outs) + [((8, 128), F32)]
        linked = len(ins) - count
        for i in ins:
            kind, array = i if isinstance(i, tuple) else (pltpu.VMEM, i)
            specs.append(pl.BlockSpec(memory_space=kind))
            operands.append(array if kind == pltpu.SMEM else pltpu.with_memory_space_constraint(array, kind))
        out_specs, shapes = [], []
        for o in outs:
            kind, shape = o if len(o) == 2 and isinstance(o[1], tuple) else (pltpu.VMEM, o)
            out_specs.append(pl.BlockSpec(memory_space=kind))
            shapes.append(kind(*shape))

        def body(*refs):
            after = count + linked
            kernel(*refs[:count], *refs[after : after + len(outs) - 1], *refs[after + len(outs) :])

        *results, self.link = pl.pallas_call(
            body,
            in_specs=specs,
            out_specs=out_specs,
            out_shape=shapes,
            scratch_shapes=list(scratch),
            input_output_aliases=alias,
            cost_estimate=pl.CostEstimate(flops=int(us * 1.15e9), bytes_accessed=0, transcendentals=0),
            compiler_params=pltpu.CompilerParams(vmem_limit_bytes=vmem << 20),
        )(*operands)
        return results


def turn(s, w, wl, wlt, raw, scratch, sem):
    copy = pltpu.make_async_copy(w.at[s, 0, 0], raw, sem)
    copy.start()
    copy.wait()
    swap_in(raw, scratch, wl)
    for leg in range(D):
        wlt[leg] = wl[leg].astype(F32).T.astype(BF16)


def prep(s, states, peps, ck, oc, start, kron, kron_t, raw, scratch, sem):
    row = lax.axis_index("row")
    sources = ((0, ck), (ROWS - 1, oc))
    for at, source in sources:

        @pl.when(row == at)
        def _():
            pltpu.make_async_copy(source.at[s, 0], raw, sem).start()

    site = jnp.where(states[s, 0, 0] == 0, peps[:, 0].astype(F32), peps[:, 1].astype(F32)).astype(BF16)
    keep = (lax.broadcasted_iota(jnp.int32, (D, 512), 0) == (lax.broadcasted_iota(jnp.int32, (D, 512), 1) & 7)).astype(F32)
    wide = picker(512, 64, lambda i, j: (i >> 3) == j)
    tall = picker(64, 512, lambda i, j: i == (j >> 3))
    rows, columns = 0.0, 0.0
    for half in range(2):
        part = site[:, 64 * half : 64 * half + 64]
        rows += mm(picker(512, 32, lambda i, j: (i >> 3) == 2 * j + half), part)
        columns += mm(part.astype(F32).T.astype(BF16), picker(32, 512, lambda i, j: 2 * i + half == (j >> 3)))
    kron_t[...] = (mm(rows.astype(BF16), tall).reshape(64, D, 512) * keep[None]).reshape(512, 512).astype(BF16)
    kron[...] = (mm(wide, columns.astype(BF16)).reshape(64, D, 512) * keep[None]).reshape(512, 512).astype(BF16)
    for at, source in sources:

        @pl.when(row == at)
        def _():
            pltpu.make_async_copy(source.at[s, 0], raw, sem).wait()
            swap_in(raw, scratch, start)


def absorb(level, *refs):
    arrived, wl, wlt, wr, kron, kron_t = refs[:6]
    x, y, xb, yb, msg = refs[-5:]
    row = lax.axis_index("row")

    @pl.when(row == level)
    def _():
        front(arrived, wlt, kron, x, y)
        close(y, wr, msg)

    @pl.when(row == ROWS - 1 - level)
    def _():
        back(arrived, wr, wl, kron_t, yb, xb, msg)


def meet(start, got0, got1, got2, wlt, kron, x_in, y_in, x, y, right, bnd, zbar):
    row = lax.axis_index("row")
    first = [start, got0, got0, start]
    second = [got2, got1, got1, got2]
    for at in range(ROWS):

        @pl.when(row == at)
        def _():
            b, z = (first, second) if at < ROWS // 2 else (second, first)
            bnd[...] = b[at][...]
            zbar[...] = z[at][...]

    @pl.when(row == ROWS - 1)
    def _():
        front(bnd, wlt, kron, x, y)

    right_grad(y, zbar, right)


def tile_work(s, states, zbar, wr, x, yb, tiles):
    @pl.when(lax.axis_index("row") == 0)
    def _():
        back_spread(zbar, wr, yb)

    tile_grad(x, yb, tiles, states[s, 0, 0])


def rest_work(s, wl, kron_t, bnd, yb, xb, msgs, left, cot, msg, scratch, out, sem):
    row = lax.axis_index("row")
    for level, source in enumerate(msgs):

        @pl.when(row == ROWS - 1 - level)
        def _():
            msg[...] = source[...]

    @pl.when(row == 0)
    def _():
        back_lift(wl, kron_t, yb, xb, msg)

    for leg in range(D):
        scratch[pl.ds(leg, CHI, stride=D), :] = msg[leg].astype(F32)
    out[...] = scratch[...].reshape(CHI, D, CHI).astype(BF16)
    copy = pltpu.make_async_copy(out, cot.at[s, 0, 0], sem)
    copy.start()
    left_grad(bnd, xb, left)
    copy.wait()


def all_grads(s, states, zbar, wr, x, wl, kron_t, bnd, msg0, msg1, msg2, xb_in, yb_in, tiles, left, cot, xb, yb, *scratch):
    tile_work(s, states, zbar, wr, x, yb, tiles)
    rest_work(s, wl, kron_t, bnd, yb, xb, (msg0, msg1, msg2), left, cot, *scratch)


def tile_part(s, states, zbar, wr, x, yb_in, before, tiles, yb):
    tile_work(s, states, zbar, wr, x, yb, tiles)
    tiles[...] += before[...]


def rest(s, wl, kron_t, bnd, yb, msg0, msg1, msg2, xb_in, cot_in, xb, left, cot, *scratch):
    rest_work(s, wl, kron_t, bnd, yb, xb, (msg0, msg1, msg2), left, cot, *scratch)


def finish(left0, left1, got0, got1, mine, other, out, peps_out, total, peps, sems):
    copies = []
    for s, (left, got) in enumerate(((left0, got0), (left1, got1))):
        turned = [got[leg].astype(F32).T for leg in range(D)]
        for half in range(2):
            for leg in range(D):
                rows = pl.ds(leg + 512 * half, CHI // 2, stride=D)
                total[s, rows, :] = left[rows, :] + turned[leg][64 * half : 64 * half + 64]
            part = pl.ds(512 * half, 512)
            copies.append(pltpu.make_async_copy(total.at[s, part], out.at[s, 0, 0, part], sems.at[2 * s + half]))
            copies[-1].start()
    peps[...] = (mine[...] + other[...]) * 0.25
    copies.append(pltpu.make_async_copy(peps, peps_out, sems.at[4]))
    copies[-1].start()
    for copy in copies:
        copy.wait()


def shards(checkpoint, peps, configs, isometries, out_cotangent):
    samples = checkpoint.shape[0]
    cols = lax.axis_size("col")
    from_right = [((i + 1) % cols, i) for i in range(cols)]
    from_left = [(i, (i + 1) % cols) for i in range(cols)]
    outer = [(0, 1), (1, 0), (2, 3), (3, 2)]
    depth = lax.axis_size("row") * lax.axis_size("batch")
    place = [(z % ROWS) * lax.axis_size("batch") + z // ROWS for z in range(depth)]
    inner = []
    for z in range(1, depth, 2):
        inner += [(place[z], place[(z + 1) % depth]), (place[(z + 1) % depth], place[z])]
    swaps = [("row", outer), (("row", "batch"), inner), ("row", outer)]
    site = jnp.swapaxes(peps.reshape(2, 32, 128), 0, 1)
    states = (pltpu.SMEM, configs)
    both = range(samples)
    call = Chain()
    dma = pltpu.SemaphoreType.DMA
    wl, wlt, wr = [None] * samples, [None] * samples, [None] * samples
    for s in both:
        wl[s], wlt[s] = call(functools.partial(turn, s), [(pltpu.HBM, isometries)], [T, T], [RAW, RELAY, dma])
        wr[s] = lax.ppermute(wl[s], "col", from_right)
    start, kron, kron_t = zip(*[
        call(functools.partial(prep, s), [states, site, (pltpu.HBM, checkpoint), (pltpu.HBM, out_cotangent)],
             [T, KRON, KRON], [RAW, RELAY, dma])
        for s in both
    ])
    stash = [[] for _ in both]
    got = [[start[s]] for s in both]
    msgs = [[] for _ in both]
    for level in range(ROWS - 1):
        for s in both:
            *stash[s], msg = call(
                functools.partial(absorb, level),
                [got[s][level], wl[s], wlt[s], wr[s], kron[s], kron_t[s]] + stash[s],
                [XS, YS, XBS, YS, T],
                alias={6 + i: i for i in range(len(stash[s]))},
            )
            msgs[s].append(msg)
            got[s].append(lax.ppermute(msg, *swaps[level]))
    moved, left = [None] * samples, [None] * samples
    rest_scratch = [pltpu.VMEM(*T), RELAY, RAW, dma]
    tile_out, left_out = ((32, 2, 128), F32), ((CHI * D, CHI), F32)
    cot_out = (pltpu.HBM, ((2, 1, 1, CHI, D, CHI), BF16))
    for s in both:
        x, y, xb, yb = stash[s]
        x, y, right, bnd, zbar = call(
            meet, got[s] + [wlt[s], kron[s], x, y], [XS, YS, T, T, T], alias={6: 0, 7: 1})
        moved[s] = lax.ppermute(right, "col", from_left)
        if s == 0:
            tiles, left[s], cot, xb, yb = call(
                functools.partial(all_grads, s),
                [states, zbar, wr[s], x, wl[s], kron_t[s], bnd] + msgs[s] + [xb, yb],
                [tile_out, left_out, cot_out, XBS, YS], rest_scratch, alias={10: 3, 11: 4})
        else:
            tiles, yb = call(
                functools.partial(tile_part, s), [states, zbar, wr[s], x, yb, tiles], [tile_out, YS], alias={4: 1})
            xb, left[s], cot = call(
                functools.partial(rest, s), [wl[s], kron_t[s], bnd, yb] + msgs[s] + [xb, (pltpu.HBM, cot)],
                [XBS, left_out, cot_out], rest_scratch, alias={7: 0, 8: 2})
    other = lax.ppermute(tiles, "batch", [(0, 1), (1, 0)])
    iso_grad, peps_grad = call(
        finish, left + moved + [tiles, other],
        [(pltpu.HBM, ((2, 1, 1, CHI * D, CHI), F32)), (pltpu.HBM, tile_out)],
        [pltpu.VMEM((2, CHI * D, CHI), F32), pltpu.VMEM(*tile_out), pltpu.SemaphoreType.DMA((5,))])
    peps_grad = jnp.swapaxes(peps_grad, 0, 1).reshape(1, 1, 2, 4096)
    return (peps_grad, iso_grad.reshape(2, 1, 1, CHI, D, CHI), cot)


def solution(mesh):
    in_specs = (
        P("batch", "col", None, None, None),
        P("row", "col", None, None),
        P("batch", "row", "col"),
        P("batch", "row", "col", None, None, None),
        P("batch", "col", None, None, None),
    )
    out_specs = (
        P("row", "col", None, None),
        P("batch", "row", "col", None, None, None),
        P("batch", "row", "col", None, None, None),
    )
    return jax.shard_map(shards, mesh=mesh, in_specs=in_specs, out_specs=out_specs, check_vma=False)
```

```python
import functools

import jax
import jax.numpy as jnp
from jax import lax
from jax.experimental import pallas as pl
from jax.experimental.pallas import tpu as pltpu
from jax.sharding import PartitionSpec as P

F32 = jnp.float32
BF16 = jnp.bfloat16
D = 8
CHI = 128
GROUPS = CHI // D
ROWS = 4
NT = (((1,), (1,)), ((), ()))


def mm(a, b):
    return jnp.dot(a, b, preferred_element_type=F32)


def mm_nt(a, b):
    return lax.dot_general(a, b, NT, preferred_element_type=F32)


def lanes(parts):
    return jnp.concatenate(parts, axis=-1)


def picker(rows, columns, rule):
    i = lax.broadcasted_iota(jnp.int32, (rows, columns), 0)
    j = lax.broadcasted_iota(jnp.int32, (rows, columns), 1)
    return rule(i, j).astype(F32).astype(BF16)


def swap_in(src, scratch, dst):
    scratch[...] = src[...].astype(F32).reshape(CHI * D, CHI)
    for leg in range(D):
        dst[leg] = scratch[pl.ds(leg, CHI, stride=D), :].astype(BF16)


def front(b, wlt, kron, x, y):
    left = wlt[...].reshape(D * CHI, CHI)
    for pair in range(D // 2):
        out = mm(left, lanes([b[2 * pair], b[2 * pair + 1]]))
        halves = [out[:, :CHI].reshape(D, GROUPS, D, CHI), out[:, CHI:].reshape(D, GROUPS, D, CHI)]
        both = jnp.concatenate(halves, axis=2).astype(BF16)
        for leg in range(D):
            x[:, leg, pair] = both[leg]

    def body(p, _):
        two = lanes([x[2 * p].reshape(512, CHI), x[2 * p + 1].reshape(512, CHI)])
        out = mm(kron[...], two).astype(BF16)
        y[2 * p] = out[:, :CHI].reshape(D, 64, CHI)
        y[2 * p + 1] = out[:, CHI:].reshape(D, 64, CHI)
        return 0

    lax.fori_loop(0, GROUPS // 2, body, 0, unroll=True)


def close(y, wr, z):
    left = lanes([y[:, r].reshape(D * CHI, CHI) for r in range(D)])
    out = mm(left, wr[...].reshape(D * CHI, CHI)).reshape(GROUPS, D, D, CHI)
    for d in range(D):
        z[d] = out[:, d].reshape(CHI, CHI).astype(BF16)


def back_spread(zbar, wr, yb):
    left = zbar[...].reshape(D * CHI, CHI)
    for pair in range(D // 2):
        out = mm_nt(left, wr[2 * pair : 2 * pair + 2].reshape(2 * CHI, CHI))
        for half in range(2):
            piece = out[:, half * CHI : (half + 1) * CHI].reshape(D, GROUPS, D, CHI)
            yb[:, 2 * pair + half] = jnp.swapaxes(piece, 0, 1).reshape(GROUPS, 64, CHI).astype(BF16)


def back_lift(wl, kron_t, yb, xb, bbar):
    for p in range(GROUPS // 2):
        two = lanes([yb[2 * p].reshape(512, CHI), yb[2 * p + 1].reshape(512, CHI)])
        out = mm(kron_t[...], two)
        halves = [out[:, :CHI].reshape(D, D, D, CHI), out[:, CHI:].reshape(D, D, D, CHI)]
        xb[:, :, 16 * p : 16 * p + 16, :] = jnp.concatenate(halves, axis=2).astype(BF16)

    left = lanes([wl[leg] for leg in range(D)])
    for pair in range(D // 2):
        right = lanes([xb[:, 2 * pair].reshape(D * CHI, CHI), xb[:, 2 * pair + 1].reshape(D * CHI, CHI)])
        out = mm(left, right).astype(BF16)
        bbar[2 * pair] = out[:, :CHI]
        bbar[2 * pair + 1] = out[:, CHI:]


def back(zbar, wr, wl, kron_t, yb, xb, bbar):
    back_spread(zbar, wr, yb)
    back_lift(wl, kron_t, yb, xb, bbar)


def right_grad(y, zbar, out_ref):
    z = zbar[...].astype(F32).reshape(D, GROUPS, D, CHI)
    z = jnp.swapaxes(z, 0, 1).reshape(D * CHI, CHI).T.astype(BF16)
    for pair in range(D // 2):
        right = lanes([y[:, 2 * pair].reshape(D * CHI, CHI), y[:, 2 * pair + 1].reshape(D * CHI, CHI)])
        out = mm(z, right).astype(BF16)
        out_ref[2 * pair] = out[:, :CHI]
        out_ref[2 * pair + 1] = out[:, CHI:]


def tile_grad(x, yb, out_ref, state):
    sub = lax.broadcasted_iota(jnp.int32, (D, 256), 0)
    keep = (sub == (lax.broadcasted_iota(jnp.int32, (D, 256), 1) & 7)).astype(F32)
    left = lanes([x[g].reshape(512, CHI) for g in range(GROUPS)])
    diagonal = []
    for half in range(2):
        right = lanes([yb[g, 4 * half : 4 * half + 4].reshape(256, CHI) for g in range(GROUPS)])
        out = mm_nt(left, right).reshape(32, 2, D, 256) * keep[None, None]
        diagonal.append([jnp.sum(out[:, odd], axis=1) for odd in range(2)])
    total = jnp.zeros((32, CHI), F32)
    for odd in range(2):
        rows = lanes([diagonal[0][odd], diagonal[1][odd]])
        high = rows.astype(BF16)
        low = (rows - high.astype(F32)).astype(BF16)
        pick = picker(512, CHI, lambda i, j: (i >> 3) + 64 * odd == j)
        total += mm(high, pick) + mm(low, pick)
    for level in range(2):
        out_ref[:, level, :] = jnp.where(state == level, total, 0.0)


def left_grad(b, xb, out_ref):
    left = lanes([b[u] for u in range(D)])
    for pair in range(D // 2):
        right = jnp.concatenate(
            [lanes([xb[leg, u] for u in range(D)]) for leg in (2 * pair, 2 * pair + 1)], axis=0
        )
        out = mm_nt(left, right)
        out_ref[pl.ds(2 * pair, CHI, stride=D), :] = out[:, :CHI]
        out_ref[pl.ds(2 * pair + 1, CHI, stride=D), :] = out[:, CHI:]


T = ((D, CHI, CHI), BF16)
XS = ((GROUPS, D, D // 2, 16, CHI), BF16)
YS = ((GROUPS, D, 64, CHI), BF16)
XBS = ((D, D, CHI, CHI), BF16)
KRON = ((512, 512), BF16)
RAW = pltpu.VMEM((CHI, D, CHI), BF16)
RELAY = pltpu.VMEM((CHI * D, CHI), F32)


class Chain:
    def __init__(self):
        self.link = None

    def __call__(self, kernel, ins, outs, scratch=(), alias=None, vmem=20, us=0.5):
        specs, operands = [], []
        alias = dict(alias or {})
        count = len(ins)
        if self.link is not None:
            ins = list(ins) + [self.link]
            alias[count] = len(outs)
        outs = list(outs) + [((8, 128), F32)]
        linked = len(ins) - count
        for i in ins:
            kind, array = i if isinstance(i, tuple) else (pltpu.VMEM, i)
            specs.append(pl.BlockSpec(memory_space=kind))
            operands.append(array if kind == pltpu.SMEM else pltpu.with_memory_space_constraint(array, kind))
        out_specs, shapes = [], []
        for o in outs:
            kind, shape = o if len(o) == 2 and isinstance(o[1], tuple) else (pltpu.VMEM, o)
            out_specs.append(pl.BlockSpec(memory_space=kind))
            shapes.append(kind(*shape))

        def body(*refs):
            after = count + linked
            kernel(*refs[:count], *refs[after : after + len(outs) - 1], *refs[after + len(outs) :])

        *results, self.link = pl.pallas_call(
            body,
            in_specs=specs,
            out_specs=out_specs,
            out_shape=shapes,
            scratch_shapes=list(scratch),
            input_output_aliases=alias,
            cost_estimate=pl.CostEstimate(flops=int(us * 1.15e9), bytes_accessed=0, transcendentals=0),
            compiler_params=pltpu.CompilerParams(vmem_limit_bytes=vmem << 20),
        )(*operands)
        return results


def turn(s, w, wl, wlt, raw, scratch, sem):
    copy = pltpu.make_async_copy(w.at[s, 0, 0], raw, sem)
    copy.start()
    copy.wait()
    swap_in(raw, scratch, wl)
    for leg in range(D):
        wlt[leg] = wl[leg].astype(F32).T.astype(BF16)


def prep(s, states, peps, ck, oc, start, kron, kron_t, raw, scratch, sem):
    row = lax.axis_index("row")
    sources = ((0, ck), (ROWS - 1, oc))
    for at, source in sources:

        @pl.when(row == at)
        def _():
            pltpu.make_async_copy(source.at[s, 0], raw, sem).start()

    site = jnp.where(states[s, 0, 0] == 0, peps[:, 0].astype(F32), peps[:, 1].astype(F32)).astype(BF16)
    keep = (lax.broadcasted_iota(jnp.int32, (D, 512), 0) == (lax.broadcasted_iota(jnp.int32, (D, 512), 1) & 7)).astype(F32)
    wide = picker(512, 64, lambda i, j: (i >> 3) == j)
    tall = picker(64, 512, lambda i, j: i == (j >> 3))
    rows, columns = 0.0, 0.0
    for half in range(2):
        part = site[:, 64 * half : 64 * half + 64]
        rows += mm(picker(512, 32, lambda i, j: (i >> 3) == 2 * j + half), part)
        columns += mm(part.astype(F32).T.astype(BF16), picker(32, 512, lambda i, j: 2 * i + half == (j >> 3)))
    kron_t[...] = (mm(rows.astype(BF16), tall).reshape(64, D, 512) * keep[None]).reshape(512, 512).astype(BF16)
    kron[...] = (mm(wide, columns.astype(BF16)).reshape(64, D, 512) * keep[None]).reshape(512, 512).astype(BF16)
    for at, source in sources:

        @pl.when(row == at)
        def _():
            pltpu.make_async_copy(source.at[s, 0], raw, sem).wait()
            swap_in(raw, scratch, start)


def absorb(level, *refs):
    arrived, wl, wlt, wr, kron, kron_t = refs[:6]
    x, y, xb, yb, msg = refs[-5:]
    row = lax.axis_index("row")

    @pl.when(row == level)
    def _():
        front(arrived, wlt, kron, x, y)
        close(y, wr, msg)

    @pl.when(row == ROWS - 1 - level)
    def _():
        back(arrived, wr, wl, kron_t, yb, xb, msg)


def meet(start, got0, got1, got2, wlt, kron, x_in, y_in, x, y, right, bnd, zbar):
    row = lax.axis_index("row")
    first = [start, got0, got0, start]
    second = [got2, got1, got1, got2]
    for at in range(ROWS):

        @pl.when(row == at)
        def _():
            b, z = (first, second) if at < ROWS // 2 else (second, first)
            bnd[...] = b[at][...]
            zbar[...] = z[at][...]

    @pl.when(row == ROWS - 1)
    def _():
        front(bnd, wlt, kron, x, y)

    right_grad(y, zbar, right)


def tile_work(s, states, zbar, wr, x, yb, tiles):
    @pl.when(lax.axis_index("row") == 0)
    def _():
        back_spread(zbar, wr, yb)

    tile_grad(x, yb, tiles, states[s, 0, 0])


def rest_work(s, wl, kron_t, bnd, yb, xb, msgs, left, cot, msg, scratch, out, sem):
    row = lax.axis_index("row")
    for level, source in enumerate(msgs):

        @pl.when(row == ROWS - 1 - level)
        def _():
            msg[...] = source[...]

    @pl.when(row == 0)
    def _():
        back_lift(wl, kron_t, yb, xb, msg)

    for leg in range(D):
        scratch[pl.ds(leg, CHI, stride=D), :] = msg[leg].astype(F32)
    out[...] = scratch[...].reshape(CHI, D, CHI).astype(BF16)
    copy = pltpu.make_async_copy(out, cot.at[s, 0, 0], sem)
    copy.start()
    left_grad(bnd, xb, left)
    copy.wait()


def all_grads(s, states, zbar, wr, x, wl, kron_t, bnd, msg0, msg1, msg2, xb_in, yb_in, tiles, left, cot, xb, yb, *scratch):
    tile_work(s, states, zbar, wr, x, yb, tiles)
    rest_work(s, wl, kron_t, bnd, yb, xb, (msg0, msg1, msg2), left, cot, *scratch)


def tile_part(s, states, zbar, wr, x, yb_in, before, tiles, yb):
    tile_work(s, states, zbar, wr, x, yb, tiles)
    tiles[...] += before[...]


def rest(s, wl, kron_t, bnd, yb, msg0, msg1, msg2, xb_in, cot_in, xb, left, cot, *scratch):
    rest_work(s, wl, kron_t, bnd, yb, xb, (msg0, msg1, msg2), left, cot, *scratch)


def finish(left0, left1, got0, got1, mine, other, out, peps_out, total, peps, sems):
    copies = []
    for s, (left, got) in enumerate(((left0, got0), (left1, got1))):
        turned = [got[leg].astype(F32).T for leg in range(D)]
        for half in range(2):
            for leg in range(D):
                rows = pl.ds(leg + 512 * half, CHI // 2, stride=D)
                total[s, rows, :] = left[rows, :] + turned[leg][64 * half : 64 * half + 64]
            part = pl.ds(512 * half, 512)
            copies.append(pltpu.make_async_copy(total.at[s, part], out.at[s, 0, 0, part], sems.at[2 * s + half]))
            copies[-1].start()
    peps[...] = (mine[...] + other[...]) * 0.25
    copies.append(pltpu.make_async_copy(peps, peps_out, sems.at[4]))
    copies[-1].start()
    for copy in copies:
        copy.wait()


def shards(checkpoint, peps, configs, isometries, out_cotangent):
    samples = checkpoint.shape[0]
    cols = lax.axis_size("col")
    from_right = [((i + 1) % cols, i) for i in range(cols)]
    from_left = [(i, (i + 1) % cols) for i in range(cols)]
    outer = [(0, 1), (1, 0), (2, 3), (3, 2)]
    depth = lax.axis_size("row") * lax.axis_size("batch")
    place = [(z % ROWS) * lax.axis_size("batch") + z // ROWS for z in range(depth)]
    inner = []
    for z in range(1, depth, 2):
        inner += [(place[z], place[(z + 1) % depth]), (place[(z + 1) % depth], place[z])]
    swaps = [("row", outer), (("row", "batch"), inner), ("row", outer)]
    site = jnp.swapaxes(peps.reshape(2, 32, 128), 0, 1)
    states = (pltpu.SMEM, configs)
    both = range(samples)
    call = Chain()
    dma = pltpu.SemaphoreType.DMA
    wl, wlt, wr = [None] * samples, [None] * samples, [None] * samples
    for s in both:
        wl[s], wlt[s] = call(functools.partial(turn, s), [(pltpu.HBM, isometries)], [T, T], [RAW, RELAY, dma])
        wr[s] = lax.ppermute(wl[s], "col", from_right)
    start, kron, kron_t = ([None] * samples for _ in range(3))
    stash, msgs, got = ([[] for _ in both] for _ in range(3))
    for level in range(ROWS - 1):
        for s in both:
            if level == 0:
                start[s], kron[s], kron_t[s] = call(
                    functools.partial(prep, s),
                    [states, site, (pltpu.HBM, checkpoint), (pltpu.HBM, out_cotangent)],
                    [T, KRON, KRON], [RAW, RELAY, dma])
                got[s] = [start[s]]
            *stash[s], msg = call(
                functools.partial(absorb, level),
                [got[s][level], wl[s], wlt[s], wr[s], kron[s], kron_t[s]] + stash[s],
                [XS, YS, XBS, YS, T],
                alias={6 + i: i for i in range(len(stash[s]))},
            )
            msgs[s].append(msg)
            got[s].append(lax.ppermute(msg, *swaps[level]))
    moved, left = [None] * samples, [None] * samples
    rest_scratch = [pltpu.VMEM(*T), RELAY, RAW, dma]
    tile_out, left_out = ((32, 2, 128), F32), ((CHI * D, CHI), F32)
    cot_out = (pltpu.HBM, ((2, 1, 1, CHI, D, CHI), BF16))
    for s in both:
        x, y, xb, yb = stash[s]
        x, y, right, bnd, zbar = call(
            meet, got[s] + [wlt[s], kron[s], x, y], [XS, YS, T, T, T], alias={6: 0, 7: 1})
        moved[s] = lax.ppermute(right, "col", from_left)
        if s == 0:
            tiles, left[s], cot, xb, yb = call(
                functools.partial(all_grads, s),
                [states, zbar, wr[s], x, wl[s], kron_t[s], bnd] + msgs[s] + [xb, yb],
                [tile_out, left_out, cot_out, XBS, YS], rest_scratch, alias={10: 3, 11: 4})
        else:
            tiles, yb = call(
                functools.partial(tile_part, s), [states, zbar, wr[s], x, yb, tiles], [tile_out, YS], alias={4: 1})
            xb, left[s], cot = call(
                functools.partial(rest, s), [wl[s], kron_t[s], bnd, yb] + msgs[s] + [xb, (pltpu.HBM, cot)],
                [XBS, left_out, cot_out], rest_scratch, alias={7: 0, 8: 2})
    other = lax.ppermute(tiles, "batch", [(0, 1), (1, 0)])
    iso_grad, peps_grad = call(
        finish, left + moved + [tiles, other],
        [(pltpu.HBM, ((2, 1, 1, CHI * D, CHI), F32)), (pltpu.HBM, tile_out)],
        [pltpu.VMEM((2, CHI * D, CHI), F32), pltpu.VMEM(*tile_out), pltpu.SemaphoreType.DMA((5,))])
    peps_grad = jnp.swapaxes(peps_grad, 0, 1).reshape(1, 1, 2, 4096)
    return (peps_grad, iso_grad.reshape(2, 1, 1, CHI, D, CHI), cot)


def solution(mesh):
    in_specs = (
        P("batch", "col", None, None, None),
        P("row", "col", None, None),
        P("batch", "row", "col"),
        P("batch", "row", "col", None, None, None),
        P("batch", "col", None, None, None),
    )
    out_specs = (
        P("row", "col", None, None),
        P("batch", "row", "col", None, None, None),
        P("batch", "row", "col", None, None, None),
    )
    return jax.shard_map(shards, mesh=mesh, in_specs=in_specs, out_specs=out_specs, check_vma=False)
```

```python
import functools

import jax
import jax.numpy as jnp
from jax import lax
from jax.experimental import pallas as pl
from jax.experimental.pallas import tpu as pltpu
from jax.sharding import PartitionSpec as P

F32 = jnp.float32
BF16 = jnp.bfloat16
D = 8
CHI = 128
GROUPS = CHI // D
ROWS = 4
NT = (((1,), (1,)), ((), ()))


def mm(a, b):
    return jnp.dot(a, b, preferred_element_type=F32)


def mm_nt(a, b):
    return lax.dot_general(a, b, NT, preferred_element_type=F32)


def lanes(parts):
    return jnp.concatenate(parts, axis=-1)


def picker(rows, columns, rule):
    i = lax.broadcasted_iota(jnp.int32, (rows, columns), 0)
    j = lax.broadcasted_iota(jnp.int32, (rows, columns), 1)
    return rule(i, j).astype(F32).astype(BF16)


def swap_in(src, scratch, dst):
    scratch[...] = src[...].astype(F32).reshape(CHI * D, CHI)
    for leg in range(D):
        dst[leg] = scratch[pl.ds(leg, CHI, stride=D), :].astype(BF16)


def front(b, wlt, kron, x, y):
    left = wlt[...].reshape(D * CHI, CHI)
    for pair in range(D // 2):
        out = mm(left, lanes([b[2 * pair], b[2 * pair + 1]]))
        halves = [out[:, :CHI].reshape(D, GROUPS, D, CHI), out[:, CHI:].reshape(D, GROUPS, D, CHI)]
        both = jnp.concatenate(halves, axis=2).astype(BF16)
        for leg in range(D):
            x[:, leg, pair] = both[leg]

    def body(p, _):
        two = lanes([x[2 * p].reshape(512, CHI), x[2 * p + 1].reshape(512, CHI)])
        out = mm(kron[...], two).astype(BF16)
        y[2 * p] = out[:, :CHI].reshape(D, 64, CHI)
        y[2 * p + 1] = out[:, CHI:].reshape(D, 64, CHI)
        return 0

    lax.fori_loop(0, GROUPS // 2, body, 0, unroll=True)


def close(y, wr, z):
    left = lanes([y[:, r].reshape(D * CHI, CHI) for r in range(D)])
    out = mm(left, wr[...].reshape(D * CHI, CHI)).reshape(GROUPS, D, D, CHI)
    for d in range(D):
        z[d] = out[:, d].reshape(CHI, CHI).astype(BF16)


def back_spread(zbar, wr, yb):
    left = zbar[...].reshape(D * CHI, CHI)
    for pair in range(D // 2):
        out = mm_nt(left, wr[2 * pair : 2 * pair + 2].reshape(2 * CHI, CHI))
        for half in range(2):
            piece = out[:, half * CHI : (half + 1) * CHI].reshape(D, GROUPS, D, CHI)
            yb[:, 2 * pair + half] = jnp.swapaxes(piece, 0, 1).reshape(GROUPS, 64, CHI).astype(BF16)


def back_lift(wl, kron_t, yb, xb, bbar):
    for p in range(GROUPS // 2):
        two = lanes([yb[2 * p].reshape(512, CHI), yb[2 * p + 1].reshape(512, CHI)])
        out = mm(kron_t[...], two)
        halves = [out[:, :CHI].reshape(D, D, D, CHI), out[:, CHI:].reshape(D, D, D, CHI)]
        xb[:, :, 16 * p : 16 * p + 16, :] = jnp.concatenate(halves, axis=2).astype(BF16)

    left = lanes([wl[leg] for leg in range(D)])
    for pair in range(D // 2):
        right = lanes([xb[:, 2 * pair].reshape(D * CHI, CHI), xb[:, 2 * pair + 1].reshape(D * CHI, CHI)])
        out = mm(left, right).astype(BF16)
        bbar[2 * pair] = out[:, :CHI]
        bbar[2 * pair + 1] = out[:, CHI:]


def back(zbar, wr, wl, kron_t, yb, xb, bbar):
    back_spread(zbar, wr, yb)
    back_lift(wl, kron_t, yb, xb, bbar)


def right_grad(y, zbar, out_ref):
    z = zbar[...].astype(F32).reshape(D, GROUPS, D, CHI)
    z = jnp.swapaxes(z, 0, 1).reshape(D * CHI, CHI).T.astype(BF16)
    for pair in range(D // 2):
        right = lanes([y[:, 2 * pair].reshape(D * CHI, CHI), y[:, 2 * pair + 1].reshape(D * CHI, CHI)])
        out = mm(z, right).astype(BF16)
        out_ref[2 * pair] = out[:, :CHI]
        out_ref[2 * pair + 1] = out[:, CHI:]


def tile_grad(x, yb, out_ref, state):
    sub = lax.broadcasted_iota(jnp.int32, (D, 256), 0)
    keep = (sub == (lax.broadcasted_iota(jnp.int32, (D, 256), 1) & 7)).astype(F32)
    left = lanes([x[g].reshape(512, CHI) for g in range(GROUPS)])
    diagonal = []
    for half in range(2):
        right = lanes([yb[g, 4 * half : 4 * half + 4].reshape(256, CHI) for g in range(GROUPS)])
        out = mm_nt(left, right).reshape(32, 2, D, 256) * keep[None, None]
        diagonal.append([jnp.sum(out[:, odd], axis=1) for odd in range(2)])
    total = jnp.zeros((32, CHI), F32)
    for odd in range(2):
        rows = lanes([diagonal[0][odd], diagonal[1][odd]])
        high = rows.astype(BF16)
        low = (rows - high.astype(F32)).astype(BF16)
        pick = picker(512, CHI, lambda i, j: (i >> 3) + 64 * odd == j)
        total += mm(high, pick) + mm(low, pick)
    for level in range(2):
        out_ref[:, level, :] = jnp.where(state == level, total, 0.0)


def left_grad(b, xb, out_ref):
    left = lanes([b[u] for u in range(D)])
    for pair in range(D // 2):
        right = jnp.concatenate(
            [lanes([xb[leg, u] for u in range(D)]) for leg in (2 * pair, 2 * pair + 1)], axis=0
        )
        out = mm_nt(left, right)
        out_ref[pl.ds(2 * pair, CHI, stride=D), :] = out[:, :CHI]
        out_ref[pl.ds(2 * pair + 1, CHI, stride=D), :] = out[:, CHI:]


T = ((D, CHI, CHI), BF16)
XS = ((GROUPS, D, D // 2, 16, CHI), BF16)
YS = ((GROUPS, D, 64, CHI), BF16)
XBS = ((D, D, CHI, CHI), BF16)
KRON = ((512, 512), BF16)
RAW = pltpu.VMEM((CHI, D, CHI), BF16)
RELAY = pltpu.VMEM((CHI * D, CHI), F32)


class Chain:
    def __init__(self):
        self.link = None

    def __call__(self, kernel, ins, outs, scratch=(), alias=None, vmem=20, us=0.5):
        specs, operands = [], []
        alias = dict(alias or {})
        count = len(ins)
        if self.link is not None:
            ins = list(ins) + [self.link]
            alias[count] = len(outs)
        outs = list(outs) + [((8, 128), F32)]
        linked = len(ins) - count
        for i in ins:
            kind, array = i if isinstance(i, tuple) else (pltpu.VMEM, i)
            specs.append(pl.BlockSpec(memory_space=kind))
            operands.append(array if kind == pltpu.SMEM else pltpu.with_memory_space_constraint(array, kind))
        out_specs, shapes = [], []
        for o in outs:
            kind, shape = o if len(o) == 2 and isinstance(o[1], tuple) else (pltpu.VMEM, o)
            out_specs.append(pl.BlockSpec(memory_space=kind))
            shapes.append(kind(*shape))

        def body(*refs):
            after = count + linked
            kernel(*refs[:count], *refs[after : after + len(outs) - 1], *refs[after + len(outs) :])

        *results, self.link = pl.pallas_call(
            body,
            in_specs=specs,
            out_specs=out_specs,
            out_shape=shapes,
            scratch_shapes=list(scratch),
            input_output_aliases=alias,
            cost_estimate=pl.CostEstimate(flops=int(us * 1.15e9), bytes_accessed=0, transcendentals=0),
            compiler_params=pltpu.CompilerParams(vmem_limit_bytes=vmem << 20),
        )(*operands)
        return results


def turn(s, w, wl, wlt, raw, scratch, sem):
    copy = pltpu.make_async_copy(w.at[s, 0, 0], raw, sem)
    copy.start()
    copy.wait()
    swap_in(raw, scratch, wl)
    for leg in range(D):
        wlt[leg] = wl[leg].astype(F32).T.astype(BF16)


def prep(s, states, peps, ck, oc, start, kron, kron_t, raw, scratch, sem):
    row = lax.axis_index("row")
    sources = ((0, ck), (ROWS - 1, oc))
    for at, source in sources:

        @pl.when(row == at)
        def _():
            pltpu.make_async_copy(source.at[s, 0], raw, sem).start()

    site = jnp.where(states[s] == 0, peps[:, 0].astype(F32), peps[:, 1].astype(F32)).astype(BF16)
    keep = (lax.broadcasted_iota(jnp.int32, (D, 512), 0) == (lax.broadcasted_iota(jnp.int32, (D, 512), 1) & 7)).astype(F32)
    wide = picker(512, 64, lambda i, j: (i >> 3) == j)
    tall = picker(64, 512, lambda i, j: i == (j >> 3))
    rows, columns = 0.0, 0.0
    for half in range(2):
        part = site[:, 64 * half : 64 * half + 64]
        rows += mm(picker(512, 32, lambda i, j: (i >> 3) == 2 * j + half), part)
        columns += mm(part.astype(F32).T.astype(BF16), picker(32, 512, lambda i, j: 2 * i + half == (j >> 3)))
    kron_t[...] = (mm(rows.astype(BF16), tall).reshape(64, D, 512) * keep[None]).reshape(512, 512).astype(BF16)
    kron[...] = (mm(wide, columns.astype(BF16)).reshape(64, D, 512) * keep[None]).reshape(512, 512).astype(BF16)
    for at, source in sources:

        @pl.when(row == at)
        def _():
            pltpu.make_async_copy(source.at[s, 0], raw, sem).wait()
            swap_in(raw, scratch, start)


def absorb(level, arrived, wlt, wr, kron, *refs):
    x, y, xb, yb = refs[-4:]
    row = lax.axis_index("row")

    @pl.when(row == level)
    def _():
        front(arrived, wlt, kron, x, y)

    @pl.when(row == ROWS - 1 - level)
    def _():
        back_spread(arrived, wr, yb)


def emit(level, wl, wr, kron_t, y, yb, xb_in, xb, msg):
    row = lax.axis_index("row")

    @pl.when(row == level)
    def _():
        close(y, wr, msg)

    @pl.when(row == ROWS - 1 - level)
    def _():
        back_lift(wl, kron_t, yb, xb, msg)


def meet(start, got0, got1, got2, wlt, kron, x_in, y_in, x, y, right, bnd, zbar):
    row = lax.axis_index("row")
    first = [start, got0, got0, start]
    second = [got2, got1, got1, got2]
    for at in range(ROWS):

        @pl.when(row == at)
        def _():
            b, z = (first, second) if at < ROWS // 2 else (second, first)
            bnd[...] = b[at][...]
            zbar[...] = z[at][...]

    @pl.when(row == ROWS - 1)
    def _():
        front(bnd, wlt, kron, x, y)

    right_grad(y, zbar, right)


def top_spread(zbar, wr, yb_in, yb):
    @pl.when(lax.axis_index("row") == 0)
    def _():
        back_spread(zbar, wr, yb)


def top_lift(wl, kron_t, yb, msg0, msg1, msg2, *refs):
    xb, msg = refs[-2:]
    row = lax.axis_index("row")
    for level, source in enumerate((msg0, msg1, msg2)):

        @pl.when(row == ROWS - 1 - level)
        def _():
            msg[...] = source[...]

    @pl.when(row == 0)
    def _():
        back_lift(wl, kron_t, yb, xb, msg)


def tile_part(s, states, x, yb, *refs):
    tile_grad(x, yb, refs[-1], states[s])
    if len(refs) == 2:
        refs[1][...] += refs[0][...]


def left_part(bnd, xb, msg, left, out, scratch):
    for leg in range(D):
        scratch[pl.ds(leg, CHI, stride=D), :] = msg[leg].astype(F32)
    out[...] = scratch[...].reshape(CHI, D, CHI).astype(BF16)
    left_grad(bnd, xb, left)


def finish(left0, left1, got0, got1, mine, other, bar0, bar1, out, peps_out, cot, total, peps, sems):
    copies = [pltpu.make_async_copy(bar, cot.at[s, 0, 0], sems.at[5 + s]) for s, bar in enumerate((bar0, bar1))]
    for copy in copies:
        copy.start()
    for s, (left, got) in enumerate(((left0, got0), (left1, got1))):
        turned = [got[leg].astype(F32).T for leg in range(D)]
        for half in range(2):
            for leg in range(D):
                rows = pl.ds(leg + 512 * half, CHI // 2, stride=D)
                total[s, rows, :] = left[rows, :] + turned[leg][64 * half : 64 * half + 64]
            part = pl.ds(512 * half, 512)
            copies.append(pltpu.make_async_copy(total.at[s, part], out.at[s, 0, 0, part], sems.at[2 * s + half]))
            copies[-1].start()
    peps[...] = (mine[...] + other[...]) * 0.25
    copies.append(pltpu.make_async_copy(peps, peps_out, sems.at[4]))
    copies[-1].start()
    for copy in copies:
        copy.wait()


def shards(checkpoint, peps, configs, isometries, out_cotangent):
    samples = checkpoint.shape[0]
    cols = lax.axis_size("col")
    from_right = [((i + 1) % cols, i) for i in range(cols)]
    from_left = [(i, (i + 1) % cols) for i in range(cols)]
    outer = [(0, 1), (1, 0), (2, 3), (3, 2)]
    depth = lax.axis_size("row") * lax.axis_size("batch")
    place = [(z % ROWS) * lax.axis_size("batch") + z // ROWS for z in range(depth)]
    inner = []
    for z in range(1, depth, 2):
        inner += [(place[z], place[(z + 1) % depth]), (place[(z + 1) % depth], place[z])]
    swaps = [("row", outer), (("row", "batch"), inner), ("row", outer)]
    site = jnp.swapaxes(peps.reshape(2, 32, 128), 0, 1)
    states = configs
    both = range(samples)
    call = Chain()
    dma = pltpu.SemaphoreType.DMA
    wl, wlt, wr = [None] * samples, [None] * samples, [None] * samples
    for s in both:
        wl[s], wlt[s] = call(functools.partial(turn, s), [(pltpu.HBM, isometries)], [T, T], [RAW, RELAY, dma])
        wr[s] = lax.ppermute(wl[s], "col", from_right)
    start, kron, kron_t = ([None] * samples for _ in range(3))
    stash, msgs, got = ([[] for _ in both] for _ in range(3))
    for level in range(ROWS - 1):
        for s in both:
            if level == 0:
                start[s], kron[s], kron_t[s] = call(
                    functools.partial(prep, s),
                    [states, site, (pltpu.HBM, checkpoint), (pltpu.HBM, out_cotangent)],
                    [T, KRON, KRON], [RAW, RELAY, dma])
                got[s] = [start[s]]
            x, y, xb, yb = call(
                functools.partial(absorb, level), [got[s][level], wlt[s], wr[s], kron[s]] + stash[s],
                [XS, YS, XBS, YS], alias={4 + i: i for i in range(len(stash[s]))})
            xb, msg = call(
                functools.partial(emit, level), [wl[s], wr[s], kron_t[s], y, yb, xb], [XBS, T], alias={5: 0})
            stash[s] = [x, y, xb, yb]
            msgs[s].append(msg)
            got[s].append(lax.ppermute(msg, *swaps[level]))
    moved, left = [None] * samples, [None] * samples
    tile_out, left_out = ((32, 2, 128), F32), ((CHI * D, CHI), F32)
    cot_out = (pltpu.HBM, ((2, 1, 1, CHI, D, CHI), BF16))
    tiles, cot = [], []
    for s in both:
        x, y, xb, yb = stash[s]
        x, y, right, bnd, zbar = call(
            meet, got[s] + [wlt[s], kron[s], x, y], [XS, YS, T, T, T], alias={6: 0, 7: 1})
        moved[s] = lax.ppermute(right, "col", from_left)
        yb, = call(top_spread, [zbar, wr[s], yb], [YS], alias={2: 0})
        tiles = call(functools.partial(tile_part, s), [states, x, yb] + tiles, [tile_out])
        xb, msg = call(top_lift, [wl[s], kron_t[s], yb] + msgs[s] + [xb] + moved[:s], [XBS, T], alias={6: 0})
        left[s], bar = call(left_part, [bnd, xb, msg], [left_out, ((CHI, D, CHI), BF16)], [RELAY])
        cot.append(bar)
    tiles = tiles[0]
    other = lax.ppermute(tiles, "batch", [(0, 1), (1, 0)])
    iso_grad, peps_grad, cot = call(
        finish, left + moved + [tiles, other] + cot,
        [(pltpu.HBM, ((2, 1, 1, CHI * D, CHI), F32)), (pltpu.HBM, tile_out), cot_out],
        [pltpu.VMEM((2, CHI * D, CHI), F32), pltpu.VMEM(*tile_out), pltpu.SemaphoreType.DMA((7,))])
    peps_grad = jnp.swapaxes(peps_grad, 0, 1).reshape(1, 1, 2, 4096)
    return (peps_grad, iso_grad.reshape(2, 1, 1, CHI, D, CHI), cot)


def solution(mesh):
    in_specs = (
        P("batch", "col", None, None, None),
        P("row", "col", None, None),
        P("batch", "row", "col"),
        P("batch", "row", "col", None, None, None),
        P("batch", "col", None, None, None),
    )
    out_specs = (
        P("row", "col", None, None),
        P("batch", "row", "col", None, None, None),
        P("batch", "row", "col", None, None, None),
    )
    return jax.shard_map(shards, mesh=mesh, in_specs=in_specs, out_specs=out_specs, check_vma=False)
```
